256 devices in a mesh: dp: 4 (over x), expert: 64 (over z, y, core).
Axes of the slice: x: 4, y: 4, z: 8, core: 2. Of those that a mesh axis runs over, the one named last changes fastest.
Arguments:
- tokens: bfloat16 [4096, 4096], P(('dp', 'expert')), may hold values from -6 to 6
- cotangent: bfloat16 [4096, 4096], P(('dp', 'expert')), may hold values from -6 to 6
- gate_prob: float32 [4096, 8], P(('dp', 'expert')), may hold values from 0.05 to 0.6
- expert_ids: int32 [4096, 8], P(('dp', 'expert')), may hold values from 0 to 63, all different within a row; in each aligned block of 16 rows (0 to 15, 16 to 31, ...) at most 3 rows name the same one
- placement: int32 [64], replicated, may hold values from 0 to 63, each once
- gate_weight: bfloat16 [64, 768, 4096], P('expert', 'dp'), may hold values from -0.09375 to 0.09375
- up_weight: bfloat16 [64, 768, 4096], P('expert', 'dp'), may hold values from -0.09375 to 0.09375
- down_weight: bfloat16 [64, 768, 4096], P('expert', 'dp'), may hold values from -0.21875 to 0.21875
Outputs:
- mixed: bfloat16 [4096, 4096], P(('dp', 'expert'))
- token_grad: bfloat16 [4096, 4096], P(('dp', 'expert'))
- gate_grad: float32 [4096, 8], P(('dp', 'expert'))
- gate_weight_grad: bfloat16 [64, 768, 4096], P('expert', 'dp')
- up_weight_grad: bfloat16 [64, 768, 4096], P('expert', 'dp')
- down_weight_grad: bfloat16 [64, 768, 4096], P('expert', 'dp')
The draws below stay inside these ranges and needn't reach their ends.
Inputs may be any that keep to these rules, and one draw needn't show every extreme that they name: `expert_ids`: in each row the 8 experts differ. In each aligned block of 16 tokens (the tokens of one device) no expert is named by more than 3 tokens, and in some blocks one is named by exactly 3. `placement`: A permutation: each slot serves exactly one expert, and no expert is replicated.
All inputs are finite; a program needn't handle non-finite values.
Results may differ from the reference program's by a relative error of at most 0.015.
Values may be sent and summed in bfloat16 or wider, within the bound.
A program may use at most 128 MiB of HBM per device.

```python
import math
import jax
import jax.numpy as jnp
import numpy as np
from jax import lax

D = 4096
FF = 768
EXPERTS = 64
TOP = 8
TOK_DEV = 16
CAP = 3
TOKENS = 4096
N_DP = 4


def steps_of(rng, shape, cuts, low, top_value):
    def one(axis_at, shards_of):
        heights = jax.random.uniform(jax.random.fold_in(jax.random.fold_in(rng, 6), axis_at), (shards_of,), jnp.float32, low / len(cuts), top_value / len(cuts))
        return jnp.repeat(jnp.exp(heights), shape[axis_at] // shards_of).reshape((-1,) + (1,) * (len(shape) - axis_at - 1))

    gain = one(*cuts[0])
    for cut in cuts[1:]:
        gain = gain * one(*cut)
    return gain


def deal_out(own_key, own, number, rows, amount, top, reach, lean):
    order = jax.random.permutation(own_key, amount)
    packed, ordinary = shares(amount, rows * top, reach, lean, True), shares(amount, rows * top, reach, lean, False)
    places = jnp.arange(amount)

    def named(sizes, offset_by):
        used = int((sizes > 0).sum())
        fixed = max(1, used // 4)
        passed = fixed + (places - fixed + offset_by * (used - fixed)) % max(1, amount - fixed)
        return jnp.zeros((amount,), jnp.int32).at[order[jnp.where(places < fixed, places, passed)]].set(jnp.asarray(sizes, jnp.int32))

    sizes = jnp.where(number % 4 == 0, named(packed, number // 4), named(ordinary, number - number // 4 - 1))
    mixed = jax.random.permutation(jax.random.fold_in(own, 3), amount)
    source_of, taker = mixed[0:amount // 2 * 2:2], mixed[1:amount // 2 * 2:2]
    room = jnp.minimum(sizes[source_of] - 1, reach - sizes[taker]) // 2
    room = jnp.where((source_of == order[0]) | (taker == order[0]) | (sizes[taker] == 0), 0, jnp.maximum(room, 0))
    passed = jax.random.randint(jax.random.fold_in(own, 4), (amount // 2,), 0, 1 << 20) % (room + 1)
    sizes = sizes.at[source_of].add(-passed).at[taker].add(passed)
    members = jnp.searchsorted(jnp.cumsum(sizes), jnp.arange(rows * top), side="right").astype(jnp.int32)
    grid = members.reshape(top, rows).T
    grid = grid[jax.random.permutation(jax.random.fold_in(own, 1), rows)]
    offset_by = jax.random.randint(jax.random.fold_in(own, 2), (rows, 1), 0, top)
    return jnp.take_along_axis(grid, (jnp.arange(top)[None, :] + offset_by) % top, axis=1)


def shares(amount, total, limit, skew, full):
    loads = [(1 << 20) // math.isqrt(rank ** skew) + 1 for rank in range(1, amount + 1)]
    largest = limit if full else min(limit, max(-(-total // amount), total * loads[0] // sum(loads)))
    least = 1 if total - largest >= amount - 1 else 0
    holding, rest = [largest] + [least] * (amount - 1), total - largest - least * (amount - 1)
    while rest > 0:
        free = [i for i in range(1, amount) if holding[i] < largest] or [i for i in range(1, amount) if holding[i] < limit]
        pool, remaining = sum([loads[i] for i in free]), rest
        for i in free:
            addition = min(limit - holding[i], max(1, remaining * loads[i] // pool), rest)
            holding[i] = holding[i] + addition
            rest = rest - addition
    return np.array(holding)


def scatter_about(rng, dims, spread, bound, shards=(), held_as=jnp.bfloat16):
    loudness = steps_of(rng, dims, shards, -0.22, 0.18) if shards else 1.0
    array = jax.random.normal(rng, dims, jnp.float32) * spread * loudness
    return jnp.minimum(jnp.maximum(array, -bound), bound).astype(held_as)


def setup_inputs(seed: int = 0) -> dict:
    seeds = jax.random.split(jax.random.key(seed), 9)
    tokens = scatter_about(seeds[0], (TOKENS, D), 1.0, 6.0, ((0, 256),))
    cotangent = scatter_about(seeds[1], (TOKENS, D), 1.0, 6.0, ((0, 256),))
    gate_prob = jnp.clip(0.05 + 0.55 * jax.random.uniform(seeds[2], (TOKENS, TOP), jnp.float32) ** steps_of(seeds[2], (TOKENS, TOP), ((0, 256),), -0.2, 0.2), 0.05, 0.6)
    expert_ids_keys = jax.random.split(jax.random.fold_in(seeds[3], 1), TOKENS // TOK_DEV)
    expert_ids_turns = jax.random.permutation(jax.random.fold_in(seeds[3], 3), TOKENS // TOK_DEV)
    expert_ids = jax.vmap(lambda own, number: deal_out(jax.random.fold_in(seeds[3], 2), own, number, TOK_DEV, EXPERTS, TOP, CAP, 2))(expert_ids_keys, expert_ids_turns).reshape((TOKENS, TOP))
    placement = jax.random.permutation(seeds[4], EXPERTS).astype(jnp.int32)
    gate_weight = scatter_about(seeds[5], (EXPERTS, FF, D), D ** -0.5, 0.09375, ((0, 64), (1, 4)))
    up_weight = scatter_about(seeds[6], (EXPERTS, FF, D), D ** -0.5, 0.09375, ((0, 64), (1, 4)))
    down_weight = scatter_about(seeds[7], (EXPERTS, FF, D), FF ** -0.5, 0.21875, ((0, 64), (1, 4)))
    return {"tokens": tokens, "cotangent": cotangent, "gate_prob": gate_prob, "expert_ids": expert_ids, "placement": placement, "gate_weight": gate_weight, "up_weight": up_weight, "down_weight": down_weight}


def gated(values):
    sigmoid_v = jax.nn.sigmoid(values)
    return values * sigmoid_v, sigmoid_v * (1.0 + values * (1.0 - sigmoid_v))


def settle(values):
    kept = lax.optimization_barrier(values.astype(jnp.bfloat16))
    return kept.astype(jnp.float32)


def rounded_sum(partial_terms):
    kept = lax.optimization_barrier(partial_terms.astype(jnp.bfloat16))
    return jnp.sum(kept.astype(jnp.float32), axis=0).astype(jnp.bfloat16)


def reference(tokens, cotangent, gate_prob, expert_ids, placement, gate_weight, up_weight, down_weight):
    pair_total = TOKENS * TOP
    most_rows = (TOKENS // TOK_DEV) * CAP
    quarter = FF // N_DP
    slot_ids = jnp.take(placement, expert_ids.reshape(-1), axis=0).astype(jnp.int32)
    one_hot = (slot_ids[:, None] == jnp.arange(EXPERTS, dtype=jnp.int32)[None, :]).astype(jnp.int32)
    earlier_count = jnp.sum((jnp.cumsum(one_hot, axis=0) - one_hot) * one_hot, axis=1).astype(jnp.int32)
    table = jnp.full((EXPERTS * most_rows,), pair_total, jnp.int32)
    table = table.at[slot_ids * most_rows + earlier_count].set(jnp.arange(pair_total, dtype=jnp.int32))
    table = table.reshape(EXPERTS, most_rows)
    zero_row = jnp.zeros((1, D), jnp.bfloat16)
    token_ext = jnp.concatenate([tokens, zero_row], axis=0)
    cot_ext = jnp.concatenate([cotangent, zero_row], axis=0)
    prob_ext = jnp.concatenate([gate_prob.reshape(-1), jnp.zeros((1,), jnp.float32)], axis=0)

    def expert_step(state_carry, inputs):
        out_acc, grad_acc, dgate_acc = state_carry
        row_pairs, w_gate, w_up, w_down = inputs
        token_idx = jnp.where(row_pairs < pair_total, row_pairs // TOP, TOKENS).astype(jnp.int32)
        routed = token_ext[token_idx].astype(jnp.float32)
        route_prob = prob_ext[row_pairs].astype(jnp.float32)
        routed_cot = cot_ext[token_idx].astype(jnp.float32)
        scaled_grad = settle(route_prob[:, None] * routed_cot)
        gate_full = w_gate.astype(jnp.float32)
        up_full = w_up.astype(jnp.float32)
        down_full = w_down.astype(jnp.float32)
        gate_pre = jnp.dot(routed, gate_full.T, preferred_element_type=jnp.float32)
        up_pre = jnp.dot(routed, up_full.T, preferred_element_type=jnp.float32)
        silu_v, slope = gated(gate_pre)
        hidden = settle(silu_v * up_pre)
        parts_out = jnp.einsum('rqf,qfd->qrd', hidden.reshape(most_rows, N_DP, quarter), down_full.reshape(N_DP, quarter, D))
        out_rows = rounded_sum(parts_out)
        d_hidden = jnp.dot(scaled_grad, down_full.T, preferred_element_type=jnp.float32)
        d_gate_pre = settle(d_hidden * up_pre * slope)
        d_up_pre = settle(d_hidden * silu_v)
        parts_back = jnp.einsum('rqf,qfd->qrd', d_gate_pre.reshape(most_rows, N_DP, quarter), gate_full.reshape(N_DP, quarter, D))
        parts_back = parts_back + jnp.einsum('rqf,qfd->qrd', d_up_pre.reshape(most_rows, N_DP, quarter), up_full.reshape(N_DP, quarter, D))
        back_rows = rounded_sum(parts_back)
        down_grad = jnp.dot(hidden.T, scaled_grad, preferred_element_type=jnp.float32).astype(jnp.bfloat16)
        gate_grad_w = jnp.dot(d_gate_pre.T, routed, preferred_element_type=jnp.float32).astype(jnp.bfloat16)
        up_grad_w = jnp.dot(d_up_pre.T, routed, preferred_element_type=jnp.float32).astype(jnp.bfloat16)
        out_value = out_rows.astype(jnp.float32)
        out_acc = out_acc.at[token_idx].add(route_prob[:, None] * out_value)
        grad_acc = grad_acc.at[token_idx].add(back_rows.astype(jnp.float32))
        dgate_acc = dgate_acc.at[row_pairs].set(jnp.sum(routed_cot * out_value, axis=1))
        return (out_acc, grad_acc, dgate_acc), (gate_grad_w, up_grad_w, down_grad)

    start = (jnp.zeros((TOKENS + 1, D), jnp.float32), jnp.zeros((TOKENS + 1, D), jnp.float32), jnp.zeros((pair_total + 1,), jnp.float32))
    finals, weight_grads = lax.scan(expert_step, start, (table, gate_weight, up_weight, down_weight))
    out_acc, grad_acc, dgate_acc = finals
    mixed = out_acc[:TOKENS].astype(jnp.bfloat16)
    token_grad = grad_acc[:TOKENS].astype(jnp.bfloat16)
    gate_grad = dgate_acc[:pair_total].reshape(TOKENS, TOP)
    return (mixed, token_grad, gate_grad, weight_grads[0], weight_grads[1], weight_grads[2])
```

```python
import jax
import jax.numpy as jnp
from jax import lax
from jax.experimental import pallas as pl
from jax.experimental.pallas import tpu as pltpu
from jax.sharding import PartitionSpec as P

CAP = 3
NX, NZ, NY, NC = 4, 8, 4, 2
MESH = pl.DeviceIdType.MESH
F32, BF16 = jnp.float32, jnp.bfloat16

TOK = 16
BLOCKS = NC * NZ
GROUP = BLOCKS * TOK
ROWS_J = BLOCKS * CAP
ROWS = NY * ROWS_J
CW = 512
SLOTS = 4


def nt(a, b):
    return lax.dot_general(a, b, (((1,), (1,)), ((), ())), preferred_element_type=F32)


def nn(a, b):
    return jnp.dot(a, b, preferred_element_type=F32)


def split3(v):
    a = v.astype(BF16)
    rest = v - a.astype(F32)
    b = rest.astype(BF16)
    return a, b, (rest - b.astype(F32)).astype(BF16)


def iota(shape, dim):
    return lax.broadcasted_iota(jnp.int32, shape, dim)


def row_parts(r):
    q = r >> 4
    j = (q >= 3).astype(jnp.int32) + (q >= 6).astype(jnp.int32) + (q >= 9).astype(jnp.int32)
    return j, q - 3 * j, r & 15


def kernel(
    x_hbm, c_hbm, p_ref, ids_ref, place_ref, wg_hbm, wu_hbm, wd_hbm,
    mixed_ref, tgrad_ref, ggrad_ref, dwg_hbm, dwu_hbm, dwd_hbm,
    zbuf, sbuf, xr, wg, wu, wd, pb, rly, fin_a, fin_b, yr, cs, cr, zs, zr, outf,
    g_acc, u_acc, d_acc, hid, dgp, dup, hid_t, dgp_t, dup_t, stage,
    meta, dmat, dmat_t, w1, w2, prow, gacc, gsend, grecv, gz_s, gz_r,
    load_sem, bar_unused,
    zss, zrs, ess, ers, yss, yrs, xss, xrs,
    bxss, bxrs, byss, byrs, bess, bers, bzss, bzrs,
    mzss, mzrs, mess, mers, gess, gers, gzss, gzrs, wsem,
):
    D = x_hbm.shape[1]
    FQ = wg_hbm.shape[0]
    NH = D // CW
    N = 2 * NH
    x = lax.axis_index("dp")
    e = lax.axis_index("expert")
    z, y, c = e // (NY * NC), (e // NC) % NY, e % NC
    right, left, opp = (x + 1) % NX, (x + 3) % NX, (x + 2) % NX

    def at_z(i):
        return {"expert": (((z + i) % NZ) * NY + y) * NC + c}

    def at_y(i):
        return {"expert": (z * NY + (y + i) % NY) * NC + c}

    other = {"expert": (z * NY + y) * NC + (1 - c)}

    def cols(k):
        return pl.ds(pl.multiple_of(k * CW, CW), CW)

    def rows(start, size):
        return pl.ds(pl.multiple_of(start, 16), size)

    def remote(src, dst, ss, rs, dev):
        return pltpu.make_async_remote_copy(
            src_ref=src, dst_ref=dst, send_sem=ss, recv_sem=rs, device_id=dev, device_id_type=MESH
        )

    mine = rows((c * NZ + z) * TOK, TOK)
    loads = [
        pltpu.make_async_copy(x_hbm, zbuf.at[mine, pl.ds(0, D)], load_sem.at[0]),
        pltpu.make_async_copy(c_hbm, zbuf.at[mine, pl.ds(D, D)], load_sem.at[1]),
        pltpu.make_async_copy(wg_hbm, wg, load_sem.at[2]),
        pltpu.make_async_copy(wu_hbm, wu, load_sem.at[3]),
        pltpu.make_async_copy(wd_hbm, wd, load_sem.at[4]),
    ]
    for cp in loads:
        cp.start()
    barrier = pltpu.get_barrier_semaphore()
    peers = [at_z(i) for i in range(1, NZ)] + [at_y(i) for i in range(1, NY)]
    peers += [other, {"dp": right}, {"dp": left}]
    for dev in peers:
        pl.semaphore_signal(barrier, inc=1, device_id=dev, device_id_type=MESH)

    ids = ids_ref[...]
    probs = p_ref[...]
    place = place_ref[...].astype(F32)
    lane64 = iota((TOK, place.shape[1]), 1)
    lane = iota((TOK, 128), 1)
    own = jnp.zeros((TOK, 128), F32)
    for k in range(8):
        slot = jnp.sum(jnp.where(ids[:, k : k + 1] == lane64, place, 0.0), axis=1, keepdims=True)
        own = jnp.where(lane == k, slot, own)
        own = jnp.where(lane == 8 + k, probs[:, k : k + 1], own)
    meta[mine, :] = own
    loads[0].wait()
    loads[1].wait()
    pl.semaphore_wait(barrier, len(peers))

    def z_copy(i, k):
        part = (mine, cols(k))
        return remote(zbuf.at[part], zbuf.at[part], zss.at[i - 1, k], zrs.at[i - 1, k], at_z(i))

    def z_wait(i, k):
        part = (rows((c * NZ + (z + NZ - i) % NZ) * TOK, TOK), cols(k))
        remote(zbuf.at[part], zbuf.at[part], zss.at[i - 1, k], zrs.at[i - 1, k], at_z(i)).wait_recv()

    def e_copy(k):
        part = (rows(c * NZ * TOK, NZ * TOK), cols(k))
        return remote(zbuf.at[part], zbuf.at[part], ess.at[k], ers.at[k], other)

    def e_wait(k):
        part = (rows((1 - c) * NZ * TOK, NZ * TOK), cols(k))
        remote(zbuf.at[part], zbuf.at[part], ess.at[k], ers.at[k], other).wait_recv()

    def y_copy(i, k):
        src = sbuf.at[rows(((y + i) % NY) * ROWS_J, ROWS_J), cols(k)]
        dst = xr.at[rows(x * ROWS + y * ROWS_J, ROWS_J), cols(k)]
        return remote(src, dst, yss.at[i - 1, k], yrs.at[i - 1, k], at_y(i))

    def y_wait(i, k):
        dst = xr.at[rows(x * ROWS + ((y + NY - i) % NY) * ROWS_J, ROWS_J), cols(k)]
        remote(dst, dst, yss.at[i - 1, k], yrs.at[i - 1, k], at_y(i)).wait_recv()

    def block(b):
        return rows(b * ROWS, ROWS)

    def x_copy(d, k):
        if d == 2:
            par = k % 2
            ref = xr.at[block((x + 3 - 2 * par) % NX), cols(k)]
            dev = {"dp": (x + 1 + 2 * par) % NX}
        else:
            ref = xr.at[block(x), cols(k)]
            dev = {"dp": left if d else right}
        return remote(ref, ref, xss.at[d, k], xrs.at[d, k], dev)

    def x_wait(d, k):
        ref = xr.at[block((left, right, opp)[d]), cols(k)]
        remote(ref, ref, xss.at[d, k], xrs.at[d, k], {"dp": right}).wait_recv()

    def slot_of(k, b):
        return pb.at[k % SLOTS, block(b)]

    def bx_copy(d, k):
        par = k % 2
        rdev, ddev = (x + 3 - 2 * par) % NX, (x + 1 + 2 * par) % NX
        if d == 0:
            src, dst, dev = slot_of(k, opp), rly.at[:, cols(k)], rdev
        elif d == 1:
            src, dst, dev = slot_of(k, rdev), fin_b.at[:, cols(k)], rdev
        else:
            src, dst, dev = slot_of(k, ddev), fin_a.at[:, cols(k)], ddev
        return remote(src, dst, bxss.at[d, k], bxrs.at[d, k], {"dp": dev})

    def by_copy(i, k):
        src = sbuf.at[rows(((y + i) % NY) * ROWS_J, ROWS_J), cols(k)]
        dst = yr.at[rows(y * ROWS_J, ROWS_J), cols(k)]
        return remote(src, dst, byss.at[i - 1, k], byrs.at[i - 1, k], at_y(i))

    def by_wait(i, k):
        dst = yr.at[rows(((y + NY - i) % NY) * ROWS_J, ROWS_J), cols(k)]
        remote(dst, dst, byss.at[i - 1, k], byrs.at[i - 1, k], at_y(i)).wait_recv()

    def be_copy(k):
        return remote(cs.at[:, cols(k)], cr.at[:, cols(k)], bess.at[k], bers.at[k], other)

    def bz_copy(i, k):
        src = zs.at[rows(((z + i) % NZ) * TOK, TOK), cols(k)]
        dst = zr.at[rows(z * TOK, TOK), cols(k)]
        return remote(src, dst, bzss.at[i - 1, k], bzrs.at[i - 1, k], at_z(i))

    def bz_wait(i, k):
        dst = zr.at[rows(((z + NZ - i) % NZ) * TOK, TOK), cols(k)]
        remote(dst, dst, bzss.at[i - 1, k], bzrs.at[i - 1, k], at_z(i)).wait_recv()

    def mz_copy(i):
        return remote(meta.at[mine], meta.at[mine], mzss.at[i - 1], mzrs.at[i - 1], at_z(i))

    me_part = rows(c * NZ * TOK, NZ * TOK)
    oth_part = rows((1 - c) * NZ * TOK, NZ * TOK)
    me_copy = remote(meta.at[me_part], meta.at[me_part], mess, mers, other)

    for i in range(1, NZ):
        mz_copy(i).start()

    def st_a(k):
        for i in (1, 7, 2, 6, 3, 5, 4):
            z_copy(i, k).start()

    st_a(0)
    st_a(1)
    for i in range(1, NZ):
        part = rows((c * NZ + (z + NZ - i) % NZ) * TOK, TOK)
        remote(meta.at[part], meta.at[part], mzss.at[i - 1], mzrs.at[i - 1], at_z(i)).wait_recv()
    me_copy.start()
    remote(meta.at[oth_part], meta.at[oth_part], mess, mers, other).wait_recv()

    info = meta[...]
    lane = iota((GROUP, 128), 1)
    target = jnp.where(lane < NY, z * (NY * NC) + c + NC * lane, -1).astype(F32)
    used = jnp.zeros((GROUP, 128), F32)
    prob = jnp.zeros((GROUP, 128), F32)
    for k in range(8):
        hit = info[:, k : k + 1] == target
        used += jnp.where(hit, 1.0, 0.0)
        prob += jnp.where(hit, info[:, 8 + k : 9 + k], 0.0)
    t_row, t_col = iota((GROUP, GROUP), 0), iota((GROUP, GROUP), 1)
    before = ((t_row >> 4) == (t_col >> 4)) & (t_col < t_row)
    used_b = used.astype(BF16)
    rank_b = nn(jnp.where(before, 1.0, 0.0).astype(BF16), used_b).astype(BF16)
    probs3 = split3(prob)
    rj, rrank, rblk = row_parts(iota((ROWS, 128), 0))
    spread = jnp.where(rj == iota((ROWS, 128), 1), 1.0, 0.0).astype(BF16)
    rj, rrank, rblk = row_parts(iota((ROWS, GROUP), 0))
    keep = (rblk == (iota((ROWS, GROUP), 1) >> 4)) & (nt(spread, rank_b) == rrank.astype(F32))
    d_f = jnp.where(keep, nt(spread, used_b), 0.0)
    dmat[...] = d_f.astype(BF16)
    weight = nt(spread, probs3[0]) + nt(spread, probs3[1]) + nt(spread, probs3[2])
    prow[...] = jnp.broadcast_to(jnp.sum(d_f * weight, axis=1, keepdims=True), prow.shape)
    rj, rrank, rblk = row_parts(iota((128, ROWS), 1))
    spread_t = jnp.where(rj == iota((128, ROWS), 0), 1.0, 0.0).astype(BF16)
    rj, rrank, rblk = row_parts(iota((GROUP, ROWS), 1))
    keep = (rblk == (iota((GROUP, ROWS), 0) >> 4)) & (nn(rank_b, spread_t) == rrank.astype(F32))
    d_t = jnp.where(keep, nn(used_b, spread_t), 0.0)
    dmat_t[...] = d_t.astype(BF16)
    weight = nn(probs3[0], spread_t) + nn(probs3[1], spread_t) + nn(probs3[2], spread_t)
    weight = d_t * weight
    w1[...] = weight.astype(BF16)
    w2[...] = (weight - weight.astype(BF16).astype(F32)).astype(BF16)

    g_acc[...] = jnp.zeros_like(g_acc)
    u_acc[...] = jnp.zeros_like(u_acc)
    d_acc[...] = jnp.zeros_like(d_acc)
    gacc[...] = jnp.zeros_like(gacc)
    loads[2].wait()
    loads[3].wait()
    loads[4].wait()

    def st_b(k):
        for i in range(1, NZ):
            z_wait(i, k)
        e_copy(k).start()

    def st_c(k):
        e_wait(k)
        scale = jnp.where(k < NH, 1.0, prow[:, 0:1])
        sbuf[:, cols(k)] = (nn(dmat[...], zbuf[:, cols(k)]) * scale).astype(BF16)
        for i in range(1, NY):
            y_copy(i, k).start()
        xr[rows(x * ROWS + y * ROWS_J, ROWS_J), cols(k)] = sbuf[rows(y * ROWS_J, ROWS_J), cols(k)]

    def st_d(k):
        for i in range(1, NY):
            y_wait(i, k)
        x_copy(0, k).start()
        x_copy(1, k).start()

    def st_e(k):
        x_wait(0, k)
        x_wait(1, k)
        x_copy(2, k).start()

    def st_f(k):
        x_wait(2, k)

        @pl.when(k < NH)
        def _():
            part = xr[:, cols(k)]
            g_acc[...] += nt(part, wg[:, cols(k)])
            u_acc[...] += nt(part, wu[:, cols(k)])

        @pl.when(k >= NH)
        def _():
            d_acc[...] += nt(xr[:, cols(k)], wd[:, cols(k - NH)])

        @pl.when(k == NH - 1)
        def _():
            def one(i, carry):
                part = rows(i * 64, 64)
                g, u = g_acc[part, :], u_acc[part, :]
                sig = 1.0 / (1.0 + jnp.exp(-g))
                silu = g * sig
                hid[part, :] = (silu * u).astype(BF16)
                g_acc[part, :] = u * (sig * (1.0 + g * (1.0 - sig)))
                u_acc[part, :] = silu
                return carry

            lax.fori_loop(0, NX * ROWS // 64, one, 0)
            hid_t[...] = hid[...].astype(F32).T.astype(BF16)

        @pl.when(k == N - 1)
        def _():
            def one(i, carry):
                part = rows(i * 64, 64)
                dh = d_acc[part, :]
                dgp[part, :] = (dh * g_acc[part, :]).astype(BF16)
                dup[part, :] = (dh * u_acc[part, :]).astype(BF16)
                return carry

            lax.fori_loop(0, NX * ROWS // 64, one, 0)

    def st_g(k):
        for i in range(1, NZ):
            z_copy(i, k).wait_send()
        e_copy(k).wait_send()
        for i in range(1, NY):
            y_copy(i, k).wait_send()
        for d in range(3):
            x_copy(d, k).wait_send()

    def st_w(k):
        for d in range(3):
            bx_copy(d, k).wait_send()

    def st_p(k):
        @pl.when(k < NH)
        def _():
            pb[k % SLOTS] = nn(hid[...], wd[:, cols(k)]).astype(BF16)

        @pl.when(k >= NH)
        def _():
            part = cols(k - NH)
            pb[k % SLOTS] = (nn(dgp[...], wg[:, part]) + nn(dup[...], wu[:, part])).astype(BF16)

        bx_copy(0, k).start()
        bx_copy(2, k).start()

    def st_q(k):
        bx_copy(0, k).wait_recv()
        ref = slot_of(k, (x + 3 - 2 * (k % 2)) % NX)
        ref[...] = (rly[:, cols(k)].astype(F32) + ref[...].astype(F32)).astype(BF16)
        bx_copy(1, k).start()

    def st_r(k):
        bx_copy(1, k).wait_recv()
        bx_copy(2, k).wait_recv()
        total = slot_of(k, x)[...].astype(F32) + fin_a[:, cols(k)].astype(F32)
        sbuf[:, cols(k)] = (total + fin_b[:, cols(k)].astype(F32)).astype(BF16)
        for i in range(1, NY):
            by_copy(i, k).start()
        yr[rows(y * ROWS_J, ROWS_J), cols(k)] = sbuf[rows(y * ROWS_J, ROWS_J), cols(k)]

    def st_s(k):
        for i in range(1, NY):
            by_wait(i, k)
        part = yr[:, cols(k)]

        @pl.when(k < NH)
        def _():
            outf[k % 2] = nn(w1[...], part) + nn(w2[...], part)
            gacc[...] += nt(zbuf[:, cols(k + NH)], part)

        @pl.when(k >= NH)
        def _():
            outf[k % 2] = nn(dmat_t[...], part)

        cs[:, cols(k)] = outf[k % 2, oth_part, :].astype(BF16)
        be_copy(k).start()

    def st_t(k):
        be_copy(k).wait_recv()
        total = outf[k % 2, me_part, :] + cr[:, cols(k)].astype(F32)
        zs[:, cols(k)] = total.astype(BF16)
        for i in (1, 7, 2, 6, 3, 5, 4):
            bz_copy(i, k).start()
        zr[rows(z * TOK, TOK), cols(k)] = zs[rows(z * TOK, TOK), cols(k)]

    def st_v(k):
        for i in range(1, NZ):
            bz_wait(i, k)
        total = zr[0:TOK, cols(k)].astype(F32)
        for i in range(1, NZ):
            total += zr[i * TOK : (i + 1) * TOK, cols(k)].astype(F32)

        @pl.when(k < NH)
        def _():
            mixed_ref[:, cols(k)] = total.astype(BF16)

        @pl.when(k >= NH)
        def _():
            tgrad_ref[:, cols(k - NH)] = total.astype(BF16)

        for i in range(1, NY):
            by_copy(i, k).wait_send()
        be_copy(k).wait_send()
        for i in range(1, NZ):
            bz_copy(i, k).wait_send()

    def w_copies(k):
        s = k % 2
        return [
            pltpu.make_async_copy(stage.at[s, n], ref.at[:, cols(k)], wsem.at[n, s])
            for n, ref in enumerate((dwg_hbm, dwu_hbm, dwd_hbm))
        ]

    def st_weights(k):
        @pl.when(k == 0)
        def _():
            dgp_t[...] = dgp[...].astype(F32).T.astype(BF16)
            dup_t[...] = dup[...].astype(F32).T.astype(BF16)

        @pl.when(k >= 2)
        def _():
            for cp in w_copies(k - 2):
                cp.wait()

        part = xr[:, cols(k)]
        stage[k % 2, 0] = nn(dgp_t[...], part).astype(BF16)
        stage[k % 2, 1] = nn(dup_t[...], part).astype(BF16)
        stage[k % 2, 2] = nn(hid_t[...], xr[:, cols(k + NH)]).astype(BF16)
        for cp in w_copies(k):
            cp.start()

    def ge_copy():
        return remote(gsend, grecv, gess, gers, other)

    def gz_copy(i):
        src = gz_s.at[rows(((z + i) % NZ) * TOK, TOK)]
        return remote(src, gz_r.at[rows(z * TOK, TOK)], gzss.at[i - 1], gzrs.at[i - 1], at_z(i))

    def st_gate():
        lanes = iota((ROWS, 128), 1)
        j, _, _ = row_parts(iota((ROWS, 128), 0))
        hit = jnp.where(lanes == z * (NY * NC) + NC * j + c, 1.0, 0.0).astype(BF16)
        a, b, d = split3(gacc[...] * dmat_t[...].astype(F32))
        outf[0, :, 0:128] = nn(a, hit) + nn(b, hit) + nn(d, hit)
        gsend[...] = outf[0, oth_part, 0:128]
        ge_copy().start()
        ge_copy().wait_recv()
        gz_s[...] = outf[0, me_part, 0:128] + grecv[...]
        for i in range(1, NZ):
            gz_copy(i).start()
        gz_r[rows(z * TOK, TOK), :] = gz_s[rows(z * TOK, TOK), :]

    def st_gate_end():
        for i in range(1, NZ):
            dst = gz_r.at[rows(((z + NZ - i) % NZ) * TOK, TOK)]
            remote(dst, dst, gzss.at[i - 1], gzrs.at[i - 1], at_z(i)).wait_recv()
        total = gz_r[0:TOK, :]
        for i in range(1, NZ):
            total += gz_r[i * TOK : (i + 1) * TOK, :]
        own = meta[mine, :]
        lanes = iota((TOK, 128), 1).astype(F32)
        lane8 = iota((TOK, 8), 1)
        res = jnp.zeros((TOK, 8), F32)
        for k in range(8):
            val = jnp.sum(jnp.where(own[:, k : k + 1] == lanes, total, 0.0), axis=1, keepdims=True)
            res = jnp.where(lane8 == k, val, res)
        ggrad_ref[...] = res
        ge_copy().wait_send()
        for i in range(1, NZ):
            gz_copy(i).wait_send()

    def guarded(fn, k, low=0, high=N):
        @pl.when((k >= low) & (k < high))
        def _():
            fn(k)

    def step(i, carry):
        guarded(st_a, i, 2)
        guarded(st_b, i - 1)
        guarded(st_c, i - 2)
        guarded(st_d, i - 3)
        guarded(st_e, i - 4)
        guarded(st_f, i - 5)
        guarded(st_g, i - 7)
        k = i - 6 - NH
        guarded(st_w, k - SLOTS)
        guarded(st_p, k)
        guarded(st_q, k - 1)
        guarded(st_r, k - 2)
        guarded(st_s, k - 3)
        guarded(st_t, k - 4)
        guarded(st_v, k - 6)
        guarded(st_weights, k - NH - 1, 0, NH)
        return carry

    lax.fori_loop(0, N + NH + 6 + 7, step, 0)
    st_gate()
    for i in range(1, NZ):
        mz_copy(i).wait_send()
    me_copy.wait_send()
    for k in (NH - 2, NH - 1):
        for cp in w_copies(k):
            cp.wait()
    st_gate_end()


def body(tokens, cotangent, gate_prob, expert_ids, placement, gate_weight, up_weight, down_weight):
    toks, D = tokens.shape
    FQ = gate_weight.shape[1]
    N = 2 * D // CW
    R = NX * ROWS
    dma = pltpu.SemaphoreType.DMA
    vm = pltpu.VMEM
    vspec = pl.BlockSpec(memory_space=pltpu.VMEM)
    aspec = pl.BlockSpec(memory_space=pl.ANY)
    scratch = [
        vm((GROUP, 2 * D), BF16),
        vm((ROWS, 2 * D), BF16),
        vm((R, 2 * D), BF16),
        vm((FQ, D), BF16), vm((FQ, D), BF16), vm((FQ, D), BF16),
        vm((SLOTS, R, CW), BF16),
        vm((ROWS, 2 * D), BF16),
        vm((ROWS, 2 * D), BF16),
        vm((ROWS, 2 * D), BF16),
        vm((ROWS, 2 * D), BF16),
        vm((NZ * TOK, 2 * D), BF16),
        vm((NZ * TOK, 2 * D), BF16),
        vm((NZ * TOK, 2 * D), BF16),
        vm((NZ * TOK, 2 * D), BF16),
        vm((2, GROUP, CW), F32),
        vm((R, FQ), F32), vm((R, FQ), F32), vm((R, FQ), F32),
        vm((R, FQ), BF16), vm((R, FQ), BF16), vm((R, FQ), BF16),
        vm((FQ, R), BF16), vm((FQ, R), BF16), vm((FQ, R), BF16),
        vm((2, 3, FQ, CW), BF16),
        vm((GROUP, 128), F32),
        vm((ROWS, GROUP), BF16),
        vm((GROUP, ROWS), BF16),
        vm((GROUP, ROWS), BF16), vm((GROUP, ROWS), BF16),
        vm((ROWS, 128), F32),
        vm((GROUP, ROWS), F32),
        vm((NZ * TOK, 128), F32), vm((NZ * TOK, 128), F32),
        vm((NZ * TOK, 128), F32), vm((NZ * TOK, 128), F32),
        dma((5,)), dma(()),
        dma((NZ - 1, N)), dma((NZ - 1, N)), dma((N,)), dma((N,)),
        dma((NY - 1, N)), dma((NY - 1, N)), dma((3, N)), dma((3, N)),
        dma((3, N)), dma((3, N)), dma((NY - 1, N)), dma((NY - 1, N)),
        dma((N,)), dma((N,)), dma((NZ - 1, N)), dma((NZ - 1, N)),
        dma((NZ - 1,)), dma((NZ - 1,)), dma(()), dma(()),
        dma(()), dma(()), dma((NZ - 1,)), dma((NZ - 1,)), dma((3, 2)),
    ]
    mixed, token_grad, gate_grad, dwg, dwu, dwd = pl.pallas_call(
        kernel,
        out_shape=(
            jax.ShapeDtypeStruct((toks, D), BF16),
            jax.ShapeDtypeStruct((toks, D), BF16),
            jax.ShapeDtypeStruct(gate_prob.shape, F32),
            jax.ShapeDtypeStruct((FQ, D), BF16),
            jax.ShapeDtypeStruct((FQ, D), BF16),
            jax.ShapeDtypeStruct((FQ, D), BF16),
        ),
        in_specs=[aspec, aspec, vspec, vspec, vspec, aspec, aspec, aspec],
        out_specs=(vspec, vspec, vspec, aspec, aspec, aspec),
        scratch_shapes=scratch,
        compiler_params=pltpu.CompilerParams(
            collective_id=0, has_side_effects=True, vmem_limit_bytes=62 * 2**20
        ),
        cost_estimate=pl.CostEstimate(
            flops=9 * 2 * R * FQ * D, bytes_accessed=6 * FQ * D * 2, transcendentals=R * FQ
        ),
        name="moe_layer",
    )(
        tokens, cotangent, gate_prob, expert_ids, placement.reshape(1, -1),
        gate_weight[0], up_weight[0], down_weight[0],
    )
    return mixed, token_grad, gate_grad, dwg[None], dwu[None], dwd[None]


def solution(mesh):
    rows_spec = P(("dp", "expert"), None)
    weight_spec = P("expert", "dp", None)
    return jax.shard_map(
        body,
        mesh=mesh,
        in_specs=(rows_spec,) * 4 + (P(),) + (weight_spec,) * 3,
        out_specs=(rows_spec,) * 3 + (weight_spec,) * 3,
        check_vma=False,
    )
```

```python
import jax
import jax.numpy as jnp
from jax import lax
from jax.experimental import pallas as pl
from jax.experimental.pallas import tpu as pltpu
from jax.sharding import PartitionSpec as P

CAP = 3
NX, NZ, NY, NC = 4, 8, 4, 2
MESH = pl.DeviceIdType.MESH
F32, BF16 = jnp.float32, jnp.bfloat16

TOK = 16
BLOCKS = NC * NZ
GROUP = BLOCKS * TOK
ROWS_J = BLOCKS * CAP
ROWS = NY * ROWS_J
CW = 512
PSLOTS = 4
SLOTS = 4
WIDE_OUT = (6, 7, 9, 11, 13, 14)
WIDE_BACK = (9, 12)


def nt(a, b):
    return lax.dot_general(a, b, (((1,), (1,)), ((), ())), preferred_element_type=F32)


def nn(a, b):
    return jnp.dot(a, b, preferred_element_type=F32)


def split3(v):
    a = v.astype(BF16)
    rest = v - a.astype(F32)
    b = rest.astype(BF16)
    return a, b, (rest - b.astype(F32)).astype(BF16)


def iota(shape, dim):
    return lax.broadcasted_iota(jnp.int32, shape, dim)


def row_parts(r):
    q = r >> 4
    j = (q >= 3).astype(jnp.int32) + (q >= 6).astype(jnp.int32) + (q >= 9).astype(jnp.int32)
    return j, q - 3 * j, r & 15


def kernel(
    x_hbm, c_hbm, own_ref, wg_hbm, wu_hbm, wd_hbm,
    mixed_ref, tgrad_ref, ggrad_ref, dwg_hbm, dwu_hbm, dwd_hbm,
    zbuf, zc, sbuf, sc, xr, wg, wu, wd, pb, rly, fin_a, fin_b, ybuf, yr, cs, cr, zs, zr,
    csc, zsc, xsc, xrc,
    g_acc, u_acc, d_acc, hid, dgp, dup, hid_t, dgp_t, dup_t, stage,
    meta, dmat, dmat_t, w1, w2, prow, gacc, gtmp, gsend, grecv, gz_s, gz_r,
    load_sem,
    zss, zrs, ess, ers, yss, yrs, xss, xrs,
    bxss, bxrs, byss, byrs, bess, bers, bzss, bzrs, wxss, wxrs, vxss, vxrs,
    mzss, mzrs, mess, mers, mxss, mxrs, gess, gers, gzss, gzrs, wsem,
):
    D = x_hbm.shape[1]
    NH = D // CW
    N = 2 * NH
    x = lax.axis_index("dp")
    e = lax.axis_index("expert")
    z, y, c = e // (NY * NC), (e // NC) % NY, e % NC
    right, left, opp = (x + 1) % NX, (x + 3) % NX, (x + 2) % NX

    def at_z(i):
        return {"expert": (((z + i) % NZ) * NY + y) * NC + c}

    def at_y(i):
        return {"expert": (z * NY + (y + i) % NY) * NC + c}

    def at_x(i):
        return {"dp": (x + i) % NX}

    other = {"expert": (z * NY + y) * NC + (1 - c)}

    def cols(k):
        return pl.ds(pl.multiple_of(k * CW, CW), CW)

    def rows(start, size):
        return pl.ds(pl.multiple_of(start, 16), size)

    def among(k, chosen):
        hit = k == chosen[0]
        for v in chosen[1:]:
            hit = hit | (k == v)
        return hit

    def place_in(k, chosen):
        return sum((k > v).astype(jnp.int32) for v in chosen)

    def either(k, chosen, wide, narrow):
        hit = among(k, chosen)

        @pl.when(hit)
        def _():
            wide(k)

        @pl.when(jnp.logical_not(hit))
        def _():
            narrow(k)

    def remote(src, dst, ss, rs, dev):
        return pltpu.make_async_remote_copy(
            src_ref=src, dst_ref=dst, send_sem=ss, recv_sem=rs, device_id=dev, device_id_type=MESH
        )

    def arrived(dst, ss, rs, dev):
        remote(dst, dst, ss, rs, dev).wait_recv()

    def all_sent(ref, sem):
        remote(ref, ref, sem, sem, {"dp": right}).wait_send()

    def all_arrived(ref, sem):
        remote(ref, ref, sem, sem, {"dp": right}).wait_recv()

    z_order = (1, 7, 2, 6, 3, 5, 4)
    seven, three = pl.ds(0, (NZ - 1) * TOK), pl.ds(0, (NY - 1) * ROWS_J)
    mine = rows((c * NZ + z) * TOK, TOK)
    me_part = rows(c * NZ * TOK, NZ * TOK)
    oth_part = rows((1 - c) * NZ * TOK, NZ * TOK)

    def z_part(i):
        return rows((c * NZ + (z + NZ - i) % NZ) * TOK, TOK)

    def y_part(i):
        return rows(((y + NY - i) % NY) * ROWS_J, ROWS_J)

    y_own = rows(y * ROWS_J, ROWS_J)

    def y_to(i):
        return rows(((y + i) % NY) * ROWS_J, ROWS_J)

    loads = [
        pltpu.make_async_copy(x_hbm, zbuf.at[mine, pl.ds(0, D)], load_sem.at[0]),
        pltpu.make_async_copy(c_hbm, zbuf.at[mine, pl.ds(D, D)], load_sem.at[1]),
        pltpu.make_async_copy(wg_hbm, wg, load_sem.at[2]),
        pltpu.make_async_copy(wu_hbm, wu, load_sem.at[3]),
        pltpu.make_async_copy(wd_hbm, wd, load_sem.at[4]),
    ]
    for cp in loads:
        cp.start()
    barrier = pltpu.get_barrier_semaphore()
    peers = [at_z(i) for i in range(1, NZ)] + [at_y(i) for i in range(1, NY)]
    peers += [at_x(i) for i in range(1, NX)] + [other]
    for dev in peers:
        pl.semaphore_signal(barrier, inc=1, device_id=dev, device_id_type=MESH)
    meta[x, mine, :] = own_ref[...]
    loads[0].wait()
    loads[1].wait()
    pl.semaphore_wait(barrier, len(peers))

    def z_copy(i, k):
        part = (mine, cols(k))
        return remote(zbuf.at[part], zbuf.at[part], zss.at[0, k], zrs.at[0, k], at_z(i))

    def e_copy(k):
        part = (me_part, cols(k))
        return remote(zbuf.at[part], zbuf.at[part], ess.at[k], ers.at[k], other)

    def y_copy(i, k):
        dst = xr.at[x, y_own, cols(k)]
        return remote(sbuf.at[k % SLOTS, y_to(i)], dst, yss.at[k], yrs.at[k], at_y(i))

    def half(k, h):
        return pl.ds(pl.multiple_of(k * CW + h * (CW // 2), CW // 2), CW // 2)

    def x_copy(d, k):
        if d < 2:
            ref = xr.at[x, :, cols(k)]
        else:
            ref = xr.at[right if d == 3 else left, :, half(k, d - 2)]
        dev = {"dp": left if d % 2 else right}
        return remote(ref, ref, xss.at[k], xrs.at[d, k], dev)

    def x_wait(d, k):
        if d < 2:
            ref = xr.at[right if d else left, :, cols(k)]
        else:
            ref = xr.at[opp, :, half(k, d - 2)]
        arrived(ref, xss.at[k], xrs.at[d, k], {"dp": right})

    def wx_copy(i, k):
        w = place_in(k, WIDE_OUT)
        dst = zc.at[w, x, mine]
        return remote(zbuf.at[mine, cols(k)], dst, wxss.at[i - 1, w], wxrs.at[i - 1, w], at_x(i))

    def wz_copy(d, s, k):
        ref = zc.at[place_in(k, WIDE_OUT), :, z_part(NZ - s if d else s)]
        return remote(ref, ref, zss.at[0, k], zrs.at[2 * s + d, k], at_z(NZ - 1 if d else 1))

    def wz_wait(d, s, k):
        ref = zc.at[place_in(k, WIDE_OUT), :, z_part(NZ - s - 1 if d else s + 1)]
        arrived(ref, zss.at[0, k], zrs.at[2 * s + d, k], at_z(1))

    z_ring = [(d, s) for s in range(4) for d in range(2)][:7]

    def we_copy(k):
        ref = zc.at[place_in(k, WIDE_OUT), :, me_part]
        return remote(ref, ref, ess.at[k], ers.at[k], other)

    def wy_copy(i, k):
        src = sc.at[place_in(k, WIDE_OUT) % 2, :, y_to(i)]
        dst = xr.at[:, y_own, cols(k)]
        return remote(src, dst, yss.at[k], yrs.at[k], at_y(i))

    def bx_copy(d, h, k):
        rdev, ddev = (right, left) if h else (left, right)
        part = pl.ds(h * (CW // 2), CW // 2)
        if d == 0:
            src, dst, dev = opp, rly, rdev
        elif d == 1:
            src, dst, dev = rdev, fin_b, rdev
        else:
            src, dst, dev = ddev, fin_a, ddev
        n = 2 * d + h
        return remote(
            pb.at[k % PSLOTS, src, :, part], dst.at[:, half(k, h)], bxss.at[k], bxrs.at[n, k], {"dp": dev}
        )

    def by_copy(i, k):
        dst = yr.at[y_own, cols(k)]
        return remote(ybuf.at[k % SLOTS, y_to(i)], dst, byss.at[k], byrs.at[k], at_y(i))

    def be_copy(k):
        return remote(cs.at[k % SLOTS], cr.at[:, cols(k)], bess.at[k], bers.at[k], other)

    def bz_copy(i, k):
        src = zs.at[k % SLOTS, rows(((z + i) % NZ) * TOK, TOK)]
        dst = zr.at[rows(z * TOK, TOK), cols(k)]
        return remote(src, dst, bzss.at[k], bzrs.at[k], at_z(i))

    W = len(WIDE_BACK)

    def v_y(k):
        return place_in(k, WIDE_BACK)

    def v_e(k, part):
        return zc.at[W + place_in(k, WIDE_BACK), :, part]

    def vy_copy(i, k):
        dst = zc.at[v_y(k), :, y_own]
        return remote(pb.at[k % PSLOTS, :, y_to(i)], dst, byss.at[k], byrs.at[k], at_y(i))

    def ve_copy(k):
        w = v_y(k)
        return remote(csc.at[w], v_e(k, pl.ds(0, NZ * TOK)), bess.at[k], bers.at[k], other)

    def vz_copy(i, k):
        src = zsc.at[v_y(k), :, rows(((z + i) % NZ) * TOK, TOK)]
        dst = v_e(k, rows(NZ * TOK + z * TOK, TOK))
        return remote(src, dst, bzss.at[k], bzrs.at[k], at_z(i))

    def vx_copy(i, k):
        w = v_y(k)
        return remote(
            xsc.at[w, (x + i) % NX], xrc.at[w, x], vxss.at[i - 1, w], vxrs.at[i - 1, w], at_x(i)
        )

    def mz_copy(i):
        ref = meta.at[x, mine]
        return remote(ref, ref, mzss.at[i - 1], mzrs.at[i - 1], at_z(i))

    me_copy = remote(meta.at[x, me_part], meta.at[x, me_part], mess, mers, other)

    def mx_copy(i):
        return remote(meta.at[x], meta.at[x], mxss.at[i - 1], mxrs.at[i - 1], at_x(i))

    def route(g, own):
        info = meta[g]
        lane = iota((GROUP, 128), 1)
        target = jnp.where(lane < NY, z * (NY * NC) + c + NC * lane, -1).astype(F32)
        used = jnp.zeros((GROUP, 128), F32)
        prob = jnp.zeros((GROUP, 128), F32)
        for k in range(8):
            hit = info[:, k : k + 1] == target
            used += jnp.where(hit, 1.0, 0.0)
            prob += jnp.where(hit, info[:, 8 + k : 9 + k], 0.0)
        t_row, t_col = iota((GROUP, GROUP), 0), iota((GROUP, GROUP), 1)
        before = ((t_row >> 4) == (t_col >> 4)) & (t_col < t_row)
        used_b = used.astype(BF16)
        rank_b = nn(jnp.where(before, 1.0, 0.0).astype(BF16), used_b).astype(BF16)
        probs3 = split3(prob)
        rj, _, _ = row_parts(iota((ROWS, 128), 0))
        spread = jnp.where(rj == iota((ROWS, 128), 1), 1.0, 0.0).astype(BF16)
        rj, rrank, rblk = row_parts(iota((ROWS, GROUP), 0))
        keep = rblk == (iota((ROWS, GROUP), 1) >> 4)
        keep = keep & (nt(spread, rank_b) == rrank.astype(F32))
        d_f = jnp.where(keep, nt(spread, used_b), 0.0)
        dmat[g] = d_f.astype(BF16)
        weight = nt(spread, probs3[0]) + nt(spread, probs3[1]) + nt(spread, probs3[2])
        prow[g] = jnp.broadcast_to(jnp.sum(d_f * weight, axis=1, keepdims=True), (ROWS, 128))
        rj, _, _ = row_parts(iota((128, ROWS), 1))
        spread_t = jnp.where(rj == iota((128, ROWS), 0), 1.0, 0.0).astype(BF16)
        rj, rrank, rblk = row_parts(iota((GROUP, ROWS), 1))
        keep = rblk == (iota((GROUP, ROWS), 0) >> 4)
        keep = keep & (nn(rank_b, spread_t) == rrank.astype(F32))
        d_t = jnp.where(keep, nn(used_b, spread_t), 0.0)
        dmat_t[g] = d_t.astype(BF16)
        if own:
            weight = nn(probs3[0], spread_t) + nn(probs3[1], spread_t) + nn(probs3[2], spread_t)
            weight = d_t * weight
            w1[...] = weight.astype(BF16)
            w2[...] = (weight - weight.astype(BF16).astype(F32)).astype(BF16)

    def route_other(i):
        @pl.when(i == 0)
        def _():
            for j in range(1, NX):
                arrived(meta.at[(x + NX - j) % NX], mxss.at[j - 1], mxrs.at[j - 1], at_x(j))

        route((x + 1 + i) % NX, False)

    def st_x(k):
        @pl.when(among(k, WIDE_OUT))
        def _():
            for i in (2, 1, 3):
                wx_copy(i, k).start()
            zc[place_in(k, WIDE_OUT), x, mine, :] = zbuf[mine, cols(k)]

    def st_a():
        def wide(k):
            w = place_in(k, WIDE_OUT)
            for i in range(1, NX):
                arrived(zc.at[w, (x + NX - i) % NX, mine], wxss.at[i - 1, w], wxrs.at[i - 1, w], at_x(i))
            wz_copy(0, 0, k).start()
            wz_copy(1, 0, k).start()

        def narrow(k):
            for i in z_order:
                z_copy(i, k).start()

        return wide, narrow

    wide_a, narrow_a = st_a()

    def st_az(k):
        @pl.when(among(k, WIDE_OUT))
        def _():
            wide_a(k)

    def st_an(k):
        @pl.when(jnp.logical_not(among(k, WIDE_OUT)))
        def _():
            narrow_a(k)

    def st_ring(s):
        def run(k):
            @pl.when(among(k, WIDE_OUT))
            def _():
                for d in range(2):
                    wz_wait(d, s - 1, k)
                    if (d, s) in z_ring:
                        wz_copy(d, s, k).start()

        return run

    def st_b(k):
        def wide(k):
            wz_wait(0, 3, k)
            we_copy(k).start()

        def narrow(k):
            all_arrived(zbuf.at[seven, cols(k)], zrs.at[0, k])
            e_copy(k).start()

        either(k, WIDE_OUT, wide, narrow)

    def st_c(k):
        def wide(k):
            w = place_in(k, WIDE_OUT)
            arrived(zc.at[w, :, oth_part], ess.at[k], ers.at[k], other)

            def one(g, carry):
                scale = jnp.where(k < NH, 1.0, prow[g, :, 0:1])
                sc[w % 2, g] = (nn(dmat[g], zc[w, g]) * scale).astype(BF16)
                return carry

            lax.fori_loop(0, NX, one, 0)
            for i in range(1, NY):
                wy_copy(i, k).start()
            xr[:, y_own, cols(k)] = sc[w % 2, :, y_own, :]

        def narrow(k):
            arrived(zbuf.at[oth_part, cols(k)], ess.at[k], ers.at[k], other)
            scale = jnp.where(k < NH, 1.0, prow[x, :, 0:1])
            sbuf[k % SLOTS] = (nn(dmat[x], zbuf[:, cols(k)]) * scale).astype(BF16)
            for i in range(1, NY):
                y_copy(i, k).start()
            xr[x, y_own, cols(k)] = sbuf[k % SLOTS, y_own, :]

        either(k, WIDE_OUT, wide, narrow)

    def st_d(k):
        @pl.when(jnp.logical_not(among(k, WIDE_OUT)))
        def _():
            all_arrived(xr.at[x, three, cols(k)], yrs.at[k])
            x_copy(0, k).start()
            x_copy(1, k).start()

    def st_e(k):
        @pl.when(jnp.logical_not(among(k, WIDE_OUT)))
        def _():
            x_wait(0, k)
            x_copy(2, k).start()
            x_wait(1, k)
            x_copy(3, k).start()

    def all_rows(k):
        return xr[:, :, cols(k)].reshape(NX * ROWS, CW)

    def st_f(k):
        def wide(k):
            all_arrived(xr.at[:, three, cols(k)], yrs.at[k])

        def narrow(k):
            x_wait(2, k)
            x_wait(3, k)

        either(k, WIDE_OUT, wide, narrow)

        @pl.when(k < NH)
        def _():
            part = all_rows(k)
            g_acc[...] += nt(part, wg[:, cols(k)])
            u_acc[...] += nt(part, wu[:, cols(k)])

        @pl.when(k >= NH)
        def _():
            d_acc[...] += nt(all_rows(k), wd[:, cols(k - NH)])

        @pl.when(k == NH - 1)
        def _():
            def one(i, carry):
                part = rows(i * 64, 64)
                g, u = g_acc[part, :], u_acc[part, :]
                sig = 1.0 / (1.0 + jnp.exp(-g))
                silu = g * sig
                hid[part, :] = (silu * u).astype(BF16)
                g_acc[part, :] = u * (sig * (1.0 + g * (1.0 - sig)))
                u_acc[part, :] = silu
                return carry

            lax.fori_loop(0, NX * ROWS // 64, one, 0)

        @pl.when(k == N - 1)
        def _():
            def one(i, carry):
                part = rows(i * 64, 64)
                dh = d_acc[part, :]
                dgp[part, :] = (dh * g_acc[part, :]).astype(BF16)
                dup[part, :] = (dh * u_acc[part, :]).astype(BF16)
                return carry

            lax.fori_loop(0, NX * ROWS // 64, one, 0)

    def st_gy(k):
        def wide(k):
            all_sent(sc.at[0, :, three], yss.at[k])

        def narrow(k):
            all_sent(sbuf.at[0, three], yss.at[k])

        either(k, WIDE_OUT, wide, narrow)

    def st_g(k):
        def wide(k):
            for i in range(1, NX):
                wx_copy(i, k).wait_send()
            all_sent(zc.at[0, :, seven], zss.at[0, k])
            we_copy(k).wait_send()

        def narrow(k):
            all_sent(zbuf.at[seven, cols(k)], zss.at[0, k])
            e_copy(k).wait_send()
            all_sent(xr.at[0:3, :, cols(k)], xss.at[k])

        either(k, WIDE_OUT, wide, narrow)

    def st_w(k):
        def wide(k):
            all_sent(sc.at[0, :, three], byss.at[k])

        def narrow(k):
            all_sent(pb.at[0, 0:3], bxss.at[k])

        either(k, WIDE_BACK, wide, narrow)

    def st_p(k):
        def store(v):
            pb[k % PSLOTS] = v.astype(BF16).reshape(NX, ROWS, CW)

        @pl.when(k < NH)
        def _():
            store(nn(hid[...], wd[:, cols(k)]))

        @pl.when(k >= NH)
        def _():
            part = cols(k - NH)
            store(nn(dgp[...], wg[:, part]) + nn(dup[...], wu[:, part]))

        def wide(k):
            for i in range(1, NY):
                vy_copy(i, k).start()
            zc[v_y(k), :, y_own, :] = pb[k % PSLOTS, :, y_own, :]

        def narrow(k):
            for d in (0, 2):
                for h in range(2):
                    bx_copy(d, h, k).start()

        either(k, WIDE_BACK, wide, narrow)

    def st_q(k):
        @pl.when(jnp.logical_not(among(k, WIDE_BACK)))
        def _():
            for h in range(2):
                bx_copy(0, h, k).wait_recv()
                part = pl.ds(h * (CW // 2), CW // 2)
                ref = pb.at[k % PSLOTS, right if h else left, :, part]
                ref[...] = (rly[:, half(k, h)].astype(F32) + ref[...].astype(F32)).astype(BF16)
                bx_copy(1, h, k).start()

    def st_r(k):
        @pl.when(jnp.logical_not(among(k, WIDE_BACK)))
        def _():
            for h in range(2):
                bx_copy(1, h, k).wait_recv()
                bx_copy(2, h, k).wait_recv()
            total = pb[k % PSLOTS, x].astype(F32) + fin_a[:, cols(k)].astype(F32)
            ybuf[k % SLOTS] = (total + fin_b[:, cols(k)].astype(F32)).astype(BF16)
            for i in range(1, NY):
                by_copy(i, k).start()
            yr[y_own, cols(k)] = ybuf[k % SLOTS, y_own, :]

    def st_s(k):
        def wide(k):
            w = v_y(k)
            all_arrived(zc.at[w, :, three], byrs.at[k])

            def one(g, carry):
                csc[w, g] = nn(dmat_t[g, oth_part, :], zc[w, g, 0:ROWS, :]).astype(BF16)
                return carry

            lax.fori_loop(0, NX, one, 0)
            ve_copy(k).start()

        def narrow(k):
            all_arrived(yr.at[three, cols(k)], byrs.at[k])
            part = yr[:, cols(k)]

            @pl.when(k < NH)
            def _():
                v = nn(w1[oth_part, :], part) + nn(w2[oth_part, :], part)
                cs[k % SLOTS] = v.astype(BF16)

                def wide_c(k):
                    gacc[...] += nt(zc[place_in(k, WIDE_OUT), x], part)

                def narrow_c(k):
                    gacc[...] += nt(zbuf[:, cols(k)], part)

                either(k + NH, WIDE_OUT, wide_c, narrow_c)

            @pl.when(k >= NH)
            def _():
                cs[k % SLOTS] = nn(dmat_t[x, oth_part, :], part).astype(BF16)

            be_copy(k).start()

        either(k, WIDE_BACK, wide, narrow)

    def st_t(k):
        def wide(k):
            w = v_y(k)
            arrived(v_e(k, pl.ds(0, NZ * TOK)), bess.at[k], bers.at[k], other)

            def one(g, carry):
                v = nn(dmat_t[g, me_part, :], zc[w, g, 0:ROWS, :])
                zsc[w, g] = (v + zc[W + w, g, 0 : NZ * TOK, :].astype(F32)).astype(BF16)
                return carry

            lax.fori_loop(0, NX, one, 0)
            for i in z_order:
                vz_copy(i, k).start()
            here = rows(NZ * TOK + z * TOK, TOK)
            zc[W + w, :, here, :] = zsc[w, :, rows(z * TOK, TOK), :]

        def narrow(k):
            be_copy(k).wait_recv()
            part = yr[:, cols(k)]

            @pl.when(k < NH)
            def _():
                v = nn(w1[me_part, :], part) + nn(w2[me_part, :], part)
                zs[k % SLOTS] = (v + cr[:, cols(k)].astype(F32)).astype(BF16)

            @pl.when(k >= NH)
            def _():
                v = nn(dmat_t[x, me_part, :], part)
                zs[k % SLOTS] = (v + cr[:, cols(k)].astype(F32)).astype(BF16)

            for i in z_order:
                bz_copy(i, k).start()
            zr[rows(z * TOK, TOK), cols(k)] = zs[k % SLOTS, rows(z * TOK, TOK), :]

        either(k, WIDE_BACK, wide, narrow)

    def z_back(i):
        return ((z + NZ - i) % NZ) * TOK

    def st_v(k):
        def wide(k):
            w = v_y(k)
            all_arrived(v_e(k, pl.ds(NZ * TOK, (NZ - 1) * TOK)), bzrs.at[k])
            total = zc[W + w, :, NZ * TOK : (NZ + 1) * TOK, :].astype(F32)
            for i in range(1, NZ):
                total += zc[W + w, :, (NZ + i) * TOK : (NZ + i + 1) * TOK, :].astype(F32)
            xsc[w] = total.astype(BF16)
            for i in (2, 1, 3):
                vx_copy(i, k).start()
            xrc[w, x] = xsc[w, x]

        def narrow(k):
            all_arrived(zr.at[seven, cols(k)], bzrs.at[k])
            total = zr[0:TOK, cols(k)].astype(F32)
            for i in range(1, NZ):
                total += zr[i * TOK : (i + 1) * TOK, cols(k)].astype(F32)

            @pl.when(k < NH)
            def _():
                mixed_ref[:, cols(k)] = total.astype(BF16)

            @pl.when(k >= NH)
            def _():
                tgrad_ref[:, cols(k - NH)] = total.astype(BF16)

        either(k, WIDE_BACK, wide, narrow)

    def st_u(k):
        @pl.when(among(k, WIDE_BACK))
        def _():
            w = v_y(k)
            for i in range(1, NX):
                part = xrc.at[w, (x + NX - i) % NX]
                arrived(part, vxss.at[i - 1, w], vxrs.at[i - 1, w], at_x(i))
            total = xrc[w, 0].astype(F32)
            for i in range(1, NX):
                total += xrc[w, i].astype(F32)
            tgrad_ref[:, cols(k - NH)] = total.astype(BF16)
            for i in range(1, NX):
                vx_copy(i, k).wait_send()

    def st_hy(k):
        @pl.when(jnp.logical_not(among(k, WIDE_BACK)))
        def _():
            all_sent(ybuf.at[0, three], byss.at[k])

    def st_he(k):
        either(k, WIDE_BACK, lambda k: ve_copy(k).wait_send(), lambda k: be_copy(k).wait_send())

    def st_hz(k):
        def wide(k):
            all_sent(zc.at[0, :, seven], bzss.at[k])

        def narrow(k):
            all_sent(zs.at[0, seven], bzss.at[k])

        either(k, WIDE_BACK, wide, narrow)

    def w_copies(k):
        return [
            pltpu.make_async_copy(stage.at[n], ref.at[:, cols(k)], wsem.at[n])
            for n, ref in enumerate((dwg_hbm, dwu_hbm, dwd_hbm))
        ]

    def st_weights(k):
        @pl.when(k == 0)
        def _():
            hid_t[...] = hid[...].astype(F32).T.astype(BF16)
            dgp_t[...] = dgp[...].astype(F32).T.astype(BF16)
            dup_t[...] = dup[...].astype(F32).T.astype(BF16)

        @pl.when(k >= 1)
        def _():
            for cp in w_copies(k - 1):
                cp.wait()

        part = all_rows(k)
        stage[0] = nn(dgp_t[...], part).astype(BF16)
        stage[1] = nn(dup_t[...], part).astype(BF16)
        stage[2] = nn(hid_t[...], all_rows(k + NH)).astype(BF16)
        for cp in w_copies(k):
            cp.start()

    def ge_copy():
        return remote(gsend, grecv, gess, gers, other)

    def gz_copy(i):
        src = gz_s.at[rows(((z + i) % NZ) * TOK, TOK)]
        return remote(src, gz_r.at[rows(z * TOK, TOK)], gzss.at[i - 1], gzrs.at[i - 1], at_z(i))

    def st_gate(k):
        lanes = iota((ROWS, 128), 1)
        j, _, _ = row_parts(iota((ROWS, 128), 0))
        hit = jnp.where(lanes == z * (NY * NC) + NC * j + c, 1.0, 0.0).astype(BF16)
        a, b, d = split3(gacc[...] * dmat_t[x].astype(F32))
        gtmp[...] = nn(a, hit) + nn(b, hit) + nn(d, hit)
        gsend[...] = gtmp[oth_part, :]
        ge_copy().start()

    def st_gate_z(k):
        ge_copy().wait_recv()
        gz_s[...] = gtmp[me_part, :] + grecv[...]
        for i in z_order:
            gz_copy(i).start()
        gz_r[rows(z * TOK, TOK), :] = gz_s[rows(z * TOK, TOK), :]

    def st_gate_end(k):
        for i in range(1, NZ):
            arrived(gz_r.at[rows(z_back(i), TOK)], gzss.at[i - 1], gzrs.at[i - 1], at_z(i))
        total = gz_r[0:TOK, :]
        for i in range(1, NZ):
            total += gz_r[i * TOK : (i + 1) * TOK, :]
        own = own_ref[...]
        lanes = iota((TOK, 128), 1).astype(F32)
        lane8 = iota((TOK, 8), 1)
        res = jnp.zeros((TOK, 8), F32)
        for k in range(8):
            val = jnp.sum(jnp.where(own[:, k : k + 1] == lanes, total, 0.0), axis=1, keepdims=True)
            res = jnp.where(lane8 == k, val, res)
        ggrad_ref[...] = res
        ge_copy().wait_send()
        for i in range(1, NZ):
            gz_copy(i).wait_send()

    def guarded(fn, k, low=0, high=N):
        @pl.when((k >= low) & (k < high))
        def _():
            fn(k)

    START = 3
    for i in z_order:
        mz_copy(i).start()
    for k in range(2):
        for i in z_order:
            z_copy(i, k).start()
    for i in range(1, NZ):
        arrived(meta.at[x, z_part(i)], mzss.at[i - 1], mzrs.at[i - 1], at_z(i))
    me_copy.start()
    g_acc[...] = jnp.zeros_like(g_acc)
    u_acc[...] = jnp.zeros_like(u_acc)
    d_acc[...] = jnp.zeros_like(d_acc)
    gacc[...] = jnp.zeros_like(gacc)
    arrived(meta.at[x, oth_part], mess, mers, other)
    for i in (2, 1, 3):
        mx_copy(i).start()
    route(x, True)
    loads[2].wait()
    loads[3].wait()
    loads[4].wait()

    def step(i, carry):
        guarded(st_x, i + 3)
        guarded(st_az, i + 2)
        guarded(st_ring(1), i + 1)
        guarded(st_ring(2), i)
        guarded(st_ring(3), i - 1)
        guarded(st_an, i - 1)
        guarded(st_gy, i - 7)
        guarded(st_d, i - 5)
        guarded(st_c, i - 4)
        guarded(st_b, i - 3)
        guarded(st_e, i - 6)
        guarded(route_other, i - 4, 0, NX - 1)
        guarded(st_f, i - 7)
        guarded(st_g, i - 10)
        k = i - 6 - NH
        guarded(st_w, k - PSLOTS)
        guarded(st_p, k)
        guarded(st_q, k - 1)
        guarded(st_hy, k - 5)
        guarded(st_r, k - 2)
        guarded(st_s, k - 4)
        guarded(st_t, k - 5)
        guarded(st_gate, k - 4 - NH, 0, 1)
        guarded(st_gate_z, k - 5 - NH, 0, 1)
        guarded(st_gate_end, k - 7 - NH, 0, 1)
        guarded(st_v, k - 7)
        guarded(st_he, k - 7)
        guarded(st_hz, k - 8)
        guarded(st_u, k - 9)
        guarded(st_weights, k - NH - 1, 0, NH)
        return carry

    lax.fori_loop(START, N + NH + 6 + 9, step, 0)
    for i in range(1, NZ):
        mz_copy(i).wait_send()
    me_copy.wait_send()
    for i in range(1, NX):
        mx_copy(i).wait_send()
    for cp in w_copies(NH - 1):
        cp.wait()


def settle(*refs):
    for i in range(len(refs) // 2):
        refs[len(refs) // 2 + i][...] = refs[i][...]


def body(tokens, cotangent, gate_prob, expert_ids, placement, gate_weight, up_weight, down_weight):
    toks, D = tokens.shape
    FQ = gate_weight.shape[1]
    N = 2 * D // CW
    R = NX * ROWS
    NT = NZ * TOK
    WO, WB = len(WIDE_OUT), len(WIDE_BACK)
    match = expert_ids[:, :, None] == jnp.arange(placement.shape[0], dtype=jnp.int32)
    slots = jnp.sum(jnp.where(match, placement, 0), axis=2).astype(F32)
    own = jnp.concatenate([slots, gate_prob, jnp.zeros((toks, 112), F32)], axis=1)
    dma = pltpu.SemaphoreType.DMA
    vm = pltpu.VMEM
    vspec = pl.BlockSpec(memory_space=pltpu.VMEM)
    aspec = pl.BlockSpec(memory_space=pl.ANY)
    scratch = [
        vm((GROUP, 2 * D), BF16),
        vm((WO, NX, GROUP, CW), BF16),
        vm((SLOTS, ROWS, CW), BF16),
        vm((2, NX, ROWS, CW), BF16),
        vm((NX, ROWS, 2 * D), BF16),
        vm((FQ, D), BF16), vm((FQ, D), BF16), vm((FQ, D), BF16),
        vm((PSLOTS, NX, ROWS, CW), BF16),
        vm((ROWS, 2 * D), BF16),
        vm((ROWS, 2 * D), BF16),
        vm((ROWS, 2 * D), BF16),
        vm((SLOTS, ROWS, CW), BF16),
        vm((ROWS, 2 * D), BF16),
        vm((SLOTS, NT, CW), BF16),
        vm((NT, 2 * D), BF16),
        vm((SLOTS, NT, CW), BF16),
        vm((NT, 2 * D), BF16),
        vm((WB, NX, NT, CW), BF16),
        vm((WB, NX, NT, CW), BF16),
        vm((WB, NX, TOK, CW), BF16),
        vm((WB, NX, TOK, CW), BF16),
        vm((R, FQ), F32), vm((R, FQ), F32), vm((R, FQ), F32),
        vm((R, FQ), BF16), vm((R, FQ), BF16), vm((R, FQ), BF16),
        vm((FQ, R), BF16), vm((FQ, R), BF16), vm((FQ, R), BF16),
        vm((3, FQ, CW), BF16),
        vm((NX, GROUP, 128), F32),
        vm((NX, ROWS, GROUP), BF16),
        vm((NX, GROUP, ROWS), BF16),
        vm((GROUP, ROWS), BF16), vm((GROUP, ROWS), BF16),
        vm((NX, ROWS, 128), F32),
        vm((GROUP, ROWS), F32),
        vm((GROUP, 128), F32),
        vm((NT, 128), F32), vm((NT, 128), F32),
        vm((NT, 128), F32), vm((NT, 128), F32),
        dma((5,)),
        dma((1, N)), dma((NZ - 1, N)), dma((N,)), dma((N,)),
        dma((N,)), dma((N,)), dma((N,)), dma((4, N)),
        dma((N,)), dma((6, N)), dma((N,)), dma((N,)),
        dma((N,)), dma((N,)), dma((N,)), dma((N,)),
        dma((NX - 1, WO)), dma((NX - 1, WO)), dma((NX - 1, WB)), dma((NX - 1, WB)),
        dma((NZ - 1,)), dma((NZ - 1,)), dma(()), dma(()), dma((NX - 1,)), dma((NX - 1,)),
        dma(()), dma(()), dma((NZ - 1,)), dma((NZ - 1,)), dma((3,)),
    ]
    shapes = (
        jax.ShapeDtypeStruct((toks, D), BF16),
        jax.ShapeDtypeStruct((toks, D), BF16),
        jax.ShapeDtypeStruct(gate_prob.shape, F32),
        jax.ShapeDtypeStruct((FQ, D), BF16),
        jax.ShapeDtypeStruct((FQ, D), BF16),
        jax.ShapeDtypeStruct((FQ, D), BF16),
    )
    outs = pl.pallas_call(
        kernel,
        out_shape=shapes,
        in_specs=[aspec, aspec, vspec, aspec, aspec, aspec],
        out_specs=(vspec, vspec, vspec, aspec, aspec, aspec),
        scratch_shapes=scratch,
        compiler_params=pltpu.CompilerParams(
            collective_id=0, has_side_effects=True, vmem_limit_bytes=63 * 2**20
        ),
        cost_estimate=pl.CostEstimate(
            flops=9 * 2 * R * FQ * D, bytes_accessed=6 * FQ * D * 2, transcendentals=R * FQ
        ),
        name="moe_layer",
    )(tokens, cotangent, own, gate_weight[0], up_weight[0], down_weight[0])
    steps = 4
    wide = pl.BlockSpec((toks, D // steps), lambda i: (0, i))
    grads = pl.BlockSpec((FQ, D // steps), lambda i: (0, i))
    specs = (wide, wide, pl.BlockSpec(gate_prob.shape, lambda i: (0, 0)), grads, grads, grads)
    outs = pl.pallas_call(
        settle, out_shape=shapes, grid=(steps,), in_specs=list(specs), out_specs=specs, name="settle"
    )(*outs)
    mixed, token_grad, gate_grad, dwg, dwu, dwd = outs
    return mixed, token_grad, gate_grad, dwg[None], dwu[None], dwd[None]


def solution(mesh):
    rows_spec = P(("dp", "expert"), None)
    weight_spec = P("expert", "dp", None)
    return jax.shard_map(
        body,
        mesh=mesh,
        in_specs=(rows_spec,) * 4 + (P(),) + (weight_spec,) * 3,
        out_specs=(rows_spec,) * 3 + (weight_spec,) * 3,
        check_vma=False,
    )
```

```python
import jax
import jax.numpy as jnp
from jax import lax
from jax.experimental import pallas as pl
from jax.experimental.pallas import tpu as pltpu
from jax.sharding import PartitionSpec as P

CAP = 3
NX, NZ, NY, NC = 4, 8, 4, 2
MESH = pl.DeviceIdType.MESH
F32, BF16 = jnp.float32, jnp.bfloat16

TOK = 16
BLOCKS = NC * NZ
GROUP = BLOCKS * TOK
ROWS_J = BLOCKS * CAP
ROWS = NY * ROWS_J
CW = 512
PSLOTS = 4
SLOTS = 4
WIDE_OUT = (6, 7, 9, 11, 13, 14)
WIDE_BACK = (9, 12)


def nt(a, b):
    return lax.dot_general(a, b, (((1,), (1,)), ((), ())), preferred_element_type=F32)


def nn(a, b):
    return jnp.dot(a, b, preferred_element_type=F32)


def split3(v):
    a = v.astype(BF16)
    rest = v - a.astype(F32)
    b = rest.astype(BF16)
    return a, b, (rest - b.astype(F32)).astype(BF16)


def iota(shape, dim):
    return lax.broadcasted_iota(jnp.int32, shape, dim)


def row_parts(r):
    q = r >> 4
    j = (q >= 3).astype(jnp.int32) + (q >= 6).astype(jnp.int32) + (q >= 9).astype(jnp.int32)
    return j, q - 3 * j, r & 15


def kernel(
    x_hbm, c_hbm, ids_ref, p_ref, place_ref, wg_hbm, wu_hbm, wd_hbm,
    mixed_ref, tgrad_ref, ggrad_ref, dwg_hbm, dwu_hbm, dwd_hbm,
    zbuf, zc, sbuf, sc, xr, wg, wu, wd, pb, rly, fin_a, fin_b, ybuf, yr, cs, cr, zs, zr,
    csc, zsc, xsc, xrc,
    g_acc, u_acc, d_acc, hid, dgp, dup, hid_t, dgp_t, dup_t, stage,
    meta, dmat, dmat_t, w1, w2, prow, gacc, gtmp, gsend, grecv, gz_s, gz_r,
    load_sem,
    zss, zrs, ess, ers, yss, yrs, xss, xrs,
    bxss, bxrs, byss, byrs, bess, bers, bzss, bzrs, wxss, wxrs, vxss, vxrs,
    mzss, mzrs, mess, mers, mxss, mxrs, gess, gers, gzss, gzrs, wsem,
):
    D = x_hbm.shape[1]
    NH = D // CW
    N = 2 * NH
    x = lax.axis_index("dp")
    e = lax.axis_index("expert")
    z, y, c = e // (NY * NC), (e // NC) % NY, e % NC
    right, left, opp = (x + 1) % NX, (x + 3) % NX, (x + 2) % NX

    def at_z(i):
        return {"expert": (((z + i) % NZ) * NY + y) * NC + c}

    def at_y(i):
        return {"expert": (z * NY + (y + i) % NY) * NC + c}

    def at_x(i):
        return {"dp": (x + i) % NX}

    other = {"expert": (z * NY + y) * NC + (1 - c)}

    def cols(k):
        return pl.ds(pl.multiple_of(k * CW, CW), CW)

    def rows(start, size):
        return pl.ds(pl.multiple_of(start, 16), size)

    def among(k, chosen):
        hit = k == chosen[0]
        for v in chosen[1:]:
            hit = hit | (k == v)
        return hit

    def place_in(k, chosen):
        return sum((k > v).astype(jnp.int32) for v in chosen)

    def either(k, chosen, wide, narrow):
        hit = among(k, chosen)

        @pl.when(hit)
        def _():
            wide(k)

        @pl.when(jnp.logical_not(hit))
        def _():
            narrow(k)

    def remote(src, dst, ss, rs, dev):
        return pltpu.make_async_remote_copy(
            src_ref=src, dst_ref=dst, send_sem=ss, recv_sem=rs, device_id=dev, device_id_type=MESH
        )

    def arrived(dst, ss, rs, dev):
        remote(dst, dst, ss, rs, dev).wait_recv()

    def all_sent(ref, sem):
        remote(ref, ref, sem, sem, {"dp": right}).wait_send()

    def all_arrived(ref, sem):
        remote(ref, ref, sem, sem, {"dp": right}).wait_recv()

    z_order = (1, 7, 2, 6, 3, 5, 4)
    seven, three = pl.ds(0, (NZ - 1) * TOK), pl.ds(0, (NY - 1) * ROWS_J)
    mine = rows((c * NZ + z) * TOK, TOK)
    me_part = rows(c * NZ * TOK, NZ * TOK)
    oth_part = rows((1 - c) * NZ * TOK, NZ * TOK)

    def z_part(i):
        return rows((c * NZ + (z + NZ - i) % NZ) * TOK, TOK)

    def y_part(i):
        return rows(((y + NY - i) % NY) * ROWS_J, ROWS_J)

    y_own = rows(y * ROWS_J, ROWS_J)

    def y_to(i):
        return rows(((y + i) % NY) * ROWS_J, ROWS_J)

    loads = [
        pltpu.make_async_copy(x_hbm, zbuf.at[mine, pl.ds(0, D)], load_sem.at[0]),
        pltpu.make_async_copy(c_hbm, zbuf.at[mine, pl.ds(D, D)], load_sem.at[1]),
        pltpu.make_async_copy(wg_hbm, wg, load_sem.at[2]),
        pltpu.make_async_copy(wu_hbm, wu, load_sem.at[3]),
        pltpu.make_async_copy(wd_hbm, wd, load_sem.at[4]),
    ]
    for cp in loads:
        cp.start()
    barrier = pltpu.get_barrier_semaphore()
    peers = [at_z(i) for i in range(1, NZ)] + [at_y(i) for i in range(1, NY)]
    peers += [at_x(i) for i in range(1, NX)] + [other]
    for dev in peers:
        pl.semaphore_signal(barrier, inc=1, device_id=dev, device_id_type=MESH)
    eye = jnp.where(iota((TOK, TOK), 0) == iota((TOK, TOK), 1), 1.0, 0.0).astype(BF16)
    ids = nt(eye, ids_ref[...].astype(F32).astype(BF16))
    p3 = split3(p_ref[...])
    probs = nt(eye, p3[0]) + nt(eye, p3[1]) + nt(eye, p3[2])
    place = place_ref[...].astype(F32)
    lane64 = iota((TOK, place.shape[1]), 1).astype(F32)
    lane = iota((TOK, 128), 1)
    own = jnp.zeros((TOK, 128), F32)
    for k in range(8):
        slot = jnp.sum(jnp.where(ids[:, k : k + 1] == lane64, place, 0.0), axis=1, keepdims=True)
        own = jnp.where(lane == k, slot, own)
        own = jnp.where(lane == 8 + k, probs[:, k : k + 1], own)
    meta[x, mine, :] = own
    loads[0].wait()
    loads[1].wait()
    pl.semaphore_wait(barrier, len(peers))

    def z_copy(i, k):
        part = (mine, cols(k))
        return remote(zbuf.at[part], zbuf.at[part], zss.at[0, k], zrs.at[0, k], at_z(i))

    def e_copy(k):
        part = (me_part, cols(k))
        return remote(zbuf.at[part], zbuf.at[part], ess.at[k], ers.at[k], other)

    def y_copy(i, k):
        dst = xr.at[x, y_own, cols(k)]
        return remote(sbuf.at[k % SLOTS, y_to(i)], dst, yss.at[k], yrs.at[k], at_y(i))

    def half(k, h):
        return pl.ds(pl.multiple_of(k * CW + h * (CW // 2), CW // 2), CW // 2)

    def x_copy(d, k):
        if d < 2:
            ref = xr.at[x, :, cols(k)]
        else:
            ref = xr.at[right if d == 3 else left, :, half(k, d - 2)]
        dev = {"dp": left if d % 2 else right}
        return remote(ref, ref, xss.at[k], xrs.at[d, k], dev)

    def x_wait(d, k):
        if d < 2:
            ref = xr.at[right if d else left, :, cols(k)]
        else:
            ref = xr.at[opp, :, half(k, d - 2)]
        arrived(ref, xss.at[k], xrs.at[d, k], {"dp": right})

    def wx_copy(i, k):
        w = place_in(k, WIDE_OUT)
        dst = zc.at[w, x, mine]
        return remote(zbuf.at[mine, cols(k)], dst, wxss.at[i - 1, w], wxrs.at[i - 1, w], at_x(i))

    def wz_copy(d, s, k):
        ref = zc.at[place_in(k, WIDE_OUT), :, z_part(NZ - s if d else s)]
        return remote(ref, ref, zss.at[0, k], zrs.at[2 * s + d, k], at_z(NZ - 1 if d else 1))

    def wz_wait(d, s, k):
        ref = zc.at[place_in(k, WIDE_OUT), :, z_part(NZ - s - 1 if d else s + 1)]
        arrived(ref, zss.at[0, k], zrs.at[2 * s + d, k], at_z(1))

    z_ring = [(d, s) for s in range(4) for d in range(2)][:7]

    def we_copy(k):
        ref = zc.at[place_in(k, WIDE_OUT), :, me_part]
        return remote(ref, ref, ess.at[k], ers.at[k], other)

    def wy_copy(i, k):
        src = sc.at[place_in(k, WIDE_OUT) % 2, :, y_to(i)]
        dst = xr.at[:, y_own, cols(k)]
        return remote(src, dst, yss.at[k], yrs.at[k], at_y(i))

    def bx_copy(d, h, k):
        rdev, ddev = (right, left) if h else (left, right)
        part = pl.ds(h * (CW // 2), CW // 2)
        if d == 0:
            src, dst, dev = opp, rly, rdev
        elif d == 1:
            src, dst, dev = rdev, fin_b, rdev
        else:
            src, dst, dev = ddev, fin_a, ddev
        n = 2 * d + h
        return remote(
            pb.at[k % PSLOTS, src, :, part], dst.at[:, half(k, h)], bxss.at[k], bxrs.at[n, k], {"dp": dev}
        )

    def by_copy(i, k):
        dst = yr.at[y_own, cols(k)]
        return remote(ybuf.at[k % SLOTS, y_to(i)], dst, byss.at[k], byrs.at[k], at_y(i))

    def be_copy(k):
        return remote(cs.at[k % SLOTS], cr.at[:, cols(k)], bess.at[k], bers.at[k], other)

    def bz_copy(i, k):
        src = zs.at[k % SLOTS, rows(((z + i) % NZ) * TOK, TOK)]
        dst = zr.at[rows(z * TOK, TOK), cols(k)]
        return remote(src, dst, bzss.at[k], bzrs.at[k], at_z(i))

    W = len(WIDE_BACK)

    def v_y(k):
        return place_in(k, WIDE_BACK)

    def v_e(k, part):
        return zc.at[W + place_in(k, WIDE_BACK), :, part]

    def vy_copy(i, k):
        dst = zc.at[v_y(k), :, y_own]
        return remote(pb.at[k % PSLOTS, :, y_to(i)], dst, byss.at[k], byrs.at[k], at_y(i))

    def ve_copy(k):
        w = v_y(k)
        return remote(csc.at[w], v_e(k, pl.ds(0, NZ * TOK)), bess.at[k], bers.at[k], other)

    def vz_copy(i, k):
        src = zsc.at[v_y(k), :, rows(((z + i) % NZ) * TOK, TOK)]
        dst = v_e(k, rows(NZ * TOK + z * TOK, TOK))
        return remote(src, dst, bzss.at[k], bzrs.at[k], at_z(i))

    def vx_copy(i, k):
        w = v_y(k)
        return remote(
            xsc.at[w, (x + i) % NX], xrc.at[w, x], vxss.at[i - 1, w], vxrs.at[i - 1, w], at_x(i)
        )

    def mz_copy(i):
        ref = meta.at[x, mine]
        return remote(ref, ref, mzss.at[i - 1], mzrs.at[i - 1], at_z(i))

    me_copy = remote(meta.at[x, me_part], meta.at[x, me_part], mess, mers, other)

    def mx_copy(i):
        return remote(meta.at[x], meta.at[x], mxss.at[i - 1], mxrs.at[i - 1], at_x(i))

    def route(g, own):
        info = meta[g]
        lane = iota((GROUP, 128), 1)
        target = jnp.where(lane < NY, z * (NY * NC) + c + NC * lane, -1).astype(F32)
        used = jnp.zeros((GROUP, 128), F32)
        prob = jnp.zeros((GROUP, 128), F32)
        for k in range(8):
            hit = info[:, k : k + 1] == target
            used += jnp.where(hit, 1.0, 0.0)
            prob += jnp.where(hit, info[:, 8 + k : 9 + k], 0.0)
        t_row, t_col = iota((GROUP, GROUP), 0), iota((GROUP, GROUP), 1)
        before = ((t_row >> 4) == (t_col >> 4)) & (t_col < t_row)
        used_b = used.astype(BF16)
        rank_b = nn(jnp.where(before, 1.0, 0.0).astype(BF16), used_b).astype(BF16)
        probs3 = split3(prob)
        rj, _, _ = row_parts(iota((ROWS, 128), 0))
        spread = jnp.where(rj == iota((ROWS, 128), 1), 1.0, 0.0).astype(BF16)
        rj, rrank, rblk = row_parts(iota((ROWS, GROUP), 0))
        keep = rblk == (iota((ROWS, GROUP), 1) >> 4)
        keep = keep & (nt(spread, rank_b) == rrank.astype(F32))
        d_f = jnp.where(keep, nt(spread, used_b), 0.0)
        dmat[g] = d_f.astype(BF16)
        weight = nt(spread, probs3[0]) + nt(spread, probs3[1]) + nt(spread, probs3[2])
        prow[g] = jnp.broadcast_to(jnp.sum(d_f * weight, axis=1, keepdims=True), (ROWS, 128))
        rj, _, _ = row_parts(iota((128, ROWS), 1))
        spread_t = jnp.where(rj == iota((128, ROWS), 0), 1.0, 0.0).astype(BF16)
        rj, rrank, rblk = row_parts(iota((GROUP, ROWS), 1))
        keep = rblk == (iota((GROUP, ROWS), 0) >> 4)
        keep = keep & (nn(rank_b, spread_t) == rrank.astype(F32))
        d_t = jnp.where(keep, nn(used_b, spread_t), 0.0)
        dmat_t[g] = d_t.astype(BF16)
        if own:
            weight = nn(probs3[0], spread_t) + nn(probs3[1], spread_t) + nn(probs3[2], spread_t)
            weight = d_t * weight
            w1[...] = weight.astype(BF16)
            w2[...] = (weight - weight.astype(BF16).astype(F32)).astype(BF16)

    def route_other(i):
        @pl.when(i == 0)
        def _():
            for j in range(1, NX):
                arrived(meta.at[(x + NX - j) % NX], mxss.at[j - 1], mxrs.at[j - 1], at_x(j))

        route((x + 1 + i) % NX, False)

    def st_x(k):
        @pl.when(among(k, WIDE_OUT))
        def _():
            for i in (2, 1, 3):
                wx_copy(i, k).start()
            zc[place_in(k, WIDE_OUT), x, mine, :] = zbuf[mine, cols(k)]

    def st_a():
        def wide(k):
            w = place_in(k, WIDE_OUT)
            for i in range(1, NX):
                arrived(zc.at[w, (x + NX - i) % NX, mine], wxss.at[i - 1, w], wxrs.at[i - 1, w], at_x(i))
            wz_copy(0, 0, k).start()
            wz_copy(1, 0, k).start()

        def narrow(k):
            for i in z_order:
                z_copy(i, k).start()

        return wide, narrow

    wide_a, narrow_a = st_a()

    def st_az(k):
        @pl.when(among(k, WIDE_OUT))
        def _():
            wide_a(k)

    def st_an(k):
        @pl.when(jnp.logical_not(among(k, WIDE_OUT)))
        def _():
            narrow_a(k)

    def st_ring(s):
        def run(k):
            @pl.when(among(k, WIDE_OUT))
            def _():
                for d in range(2):
                    wz_wait(d, s - 1, k)
                    if (d, s) in z_ring:
                        wz_copy(d, s, k).start()

        return run

    def st_b(k):
        def wide(k):
            wz_wait(0, 3, k)
            we_copy(k).start()

        def narrow(k):
            all_arrived(zbuf.at[seven, cols(k)], zrs.at[0, k])
            e_copy(k).start()

        either(k, WIDE_OUT, wide, narrow)

    def st_c(k):
        def wide(k):
            w = place_in(k, WIDE_OUT)
            arrived(zc.at[w, :, oth_part], ess.at[k], ers.at[k], other)

            def one(g, carry):
                scale = jnp.where(k < NH, 1.0, prow[g, :, 0:1])
                sc[w % 2, g] = (nn(dmat[g], zc[w, g]) * scale).astype(BF16)
                return carry

            lax.fori_loop(0, NX, one, 0)
            for i in range(1, NY):
                wy_copy(i, k).start()
            xr[:, y_own, cols(k)] = sc[w % 2, :, y_own, :]

        def narrow(k):
            arrived(zbuf.at[oth_part, cols(k)], ess.at[k], ers.at[k], other)
            scale = jnp.where(k < NH, 1.0, prow[x, :, 0:1])
            sbuf[k % SLOTS] = (nn(dmat[x], zbuf[:, cols(k)]) * scale).astype(BF16)
            for i in range(1, NY):
                y_copy(i, k).start()
            xr[x, y_own, cols(k)] = sbuf[k % SLOTS, y_own, :]

        either(k, WIDE_OUT, wide, narrow)

    def st_d(k):
        @pl.when(jnp.logical_not(among(k, WIDE_OUT)))
        def _():
            all_arrived(xr.at[x, three, cols(k)], yrs.at[k])
            x_copy(0, k).start()
            x_copy(1, k).start()

    def st_e(k):
        @pl.when(jnp.logical_not(among(k, WIDE_OUT)))
        def _():
            x_wait(0, k)
            x_copy(2, k).start()
            x_wait(1, k)
            x_copy(3, k).start()

    def all_rows(k):
        return xr[:, :, cols(k)].reshape(NX * ROWS, CW)

    def st_f(k):
        def wide(k):
            all_arrived(xr.at[:, three, cols(k)], yrs.at[k])

        def narrow(k):
            x_wait(2, k)
            x_wait(3, k)

        either(k, WIDE_OUT, wide, narrow)

        @pl.when(k < NH)
        def _():
            part = all_rows(k)
            g_acc[...] += nt(part, wg[:, cols(k)])
            u_acc[...] += nt(part, wu[:, cols(k)])

        @pl.when(k >= NH)
        def _():
            d_acc[...] += nt(all_rows(k), wd[:, cols(k - NH)])

        @pl.when(k == NH - 1)
        def _():
            def one(i, carry):
                part = rows(i * 64, 64)
                g, u = g_acc[part, :], u_acc[part, :]
                sig = 1.0 / (1.0 + jnp.exp(-g))
                silu = g * sig
                hid[part, :] = (silu * u).astype(BF16)
                g_acc[part, :] = u * (sig * (1.0 + g * (1.0 - sig)))
                u_acc[part, :] = silu
                return carry

            lax.fori_loop(0, NX * ROWS // 64, one, 0)

        @pl.when(k == N - 1)
        def _():
            def one(i, carry):
                part = rows(i * 64, 64)
                dh = d_acc[part, :]
                dgp[part, :] = (dh * g_acc[part, :]).astype(BF16)
                dup[part, :] = (dh * u_acc[part, :]).astype(BF16)
                return carry

            lax.fori_loop(0, NX * ROWS // 64, one, 0)

    def st_gy(k):
        def wide(k):
            all_sent(sc.at[0, :, three], yss.at[k])

        def narrow(k):
            all_sent(sbuf.at[0, three], yss.at[k])

        either(k, WIDE_OUT, wide, narrow)

    def st_g(k):
        def wide(k):
            for i in range(1, NX):
                wx_copy(i, k).wait_send()
            all_sent(zc.at[0, :, seven], zss.at[0, k])
            we_copy(k).wait_send()

        def narrow(k):
            all_sent(zbuf.at[seven, cols(k)], zss.at[0, k])
            e_copy(k).wait_send()
            all_sent(xr.at[0:3, :, cols(k)], xss.at[k])

        either(k, WIDE_OUT, wide, narrow)

    def st_w(k):
        def wide(k):
            all_sent(sc.at[0, :, three], byss.at[k])

        def narrow(k):
            all_sent(pb.at[0, 0:3], bxss.at[k])

        either(k, WIDE_BACK, wide, narrow)

    def st_p(k):
        def store(v):
            pb[k % PSLOTS] = v.astype(BF16).reshape(NX, ROWS, CW)

        @pl.when(k < NH)
        def _():
            store(nn(hid[...], wd[:, cols(k)]))

        @pl.when(k >= NH)
        def _():
            part = cols(k - NH)
            store(nn(dgp[...], wg[:, part]) + nn(dup[...], wu[:, part]))

        def wide(k):
            for i in range(1, NY):
                vy_copy(i, k).start()
            zc[v_y(k), :, y_own, :] = pb[k % PSLOTS, :, y_own, :]

        def narrow(k):
            for d in (0, 2):
                for h in range(2):
                    bx_copy(d, h, k).start()

        either(k, WIDE_BACK, wide, narrow)

    def st_q(k):
        @pl.when(jnp.logical_not(among(k, WIDE_BACK)))
        def _():
            for h in range(2):
                bx_copy(0, h, k).wait_recv()
                part = pl.ds(h * (CW // 2), CW // 2)
                ref = pb.at[k % PSLOTS, right if h else left, :, part]
                ref[...] = (rly[:, half(k, h)].astype(F32) + ref[...].astype(F32)).astype(BF16)
                bx_copy(1, h, k).start()

    def st_r(k):
        @pl.when(jnp.logical_not(among(k, WIDE_BACK)))
        def _():
            for h in range(2):
                bx_copy(1, h, k).wait_recv()
                bx_copy(2, h, k).wait_recv()
            total = pb[k % PSLOTS, x].astype(F32) + fin_a[:, cols(k)].astype(F32)
            ybuf[k % SLOTS] = (total + fin_b[:, cols(k)].astype(F32)).astype(BF16)
            for i in range(1, NY):
                by_copy(i, k).start()
            yr[y_own, cols(k)] = ybuf[k % SLOTS, y_own, :]

    def st_s(k):
        def wide(k):
            w = v_y(k)
            all_arrived(zc.at[w, :, three], byrs.at[k])

            def one(g, carry):
                csc[w, g] = nn(dmat_t[g, oth_part, :], zc[w, g, 0:ROWS, :]).astype(BF16)
                return carry

            lax.fori_loop(0, NX, one, 0)
            ve_copy(k).start()

        def narrow(k):
            all_arrived(yr.at[three, cols(k)], byrs.at[k])
            part = yr[:, cols(k)]

            @pl.when(k < NH)
            def _():
                v = nn(w1[oth_part, :], part) + nn(w2[oth_part, :], part)
                cs[k % SLOTS] = v.astype(BF16)

                def wide_c(k):
                    gacc[...] += nt(zc[place_in(k, WIDE_OUT), x], part)

                def narrow_c(k):
                    gacc[...] += nt(zbuf[:, cols(k)], part)

                either(k + NH, WIDE_OUT, wide_c, narrow_c)

            @pl.when(k >= NH)
            def _():
                cs[k % SLOTS] = nn(dmat_t[x, oth_part, :], part).astype(BF16)

            be_copy(k).start()

        either(k, WIDE_BACK, wide, narrow)

    def st_t(k):
        def wide(k):
            w = v_y(k)
            arrived(v_e(k, pl.ds(0, NZ * TOK)), bess.at[k], bers.at[k], other)

            def one(g, carry):
                v = nn(dmat_t[g, me_part, :], zc[w, g, 0:ROWS, :])
                zsc[w, g] = (v + zc[W + w, g, 0 : NZ * TOK, :].astype(F32)).astype(BF16)
                return carry

            lax.fori_loop(0, NX, one, 0)
            for i in z_order:
                vz_copy(i, k).start()
            here = rows(NZ * TOK + z * TOK, TOK)
            zc[W + w, :, here, :] = zsc[w, :, rows(z * TOK, TOK), :]

        def narrow(k):
            be_copy(k).wait_recv()
            part = yr[:, cols(k)]

            @pl.when(k < NH)
            def _():
                v = nn(w1[me_part, :], part) + nn(w2[me_part, :], part)
                zs[k % SLOTS] = (v + cr[:, cols(k)].astype(F32)).astype(BF16)

            @pl.when(k >= NH)
            def _():
                v = nn(dmat_t[x, me_part, :], part)
                zs[k % SLOTS] = (v + cr[:, cols(k)].astype(F32)).astype(BF16)

            for i in z_order:
                bz_copy(i, k).start()
            zr[rows(z * TOK, TOK), cols(k)] = zs[k % SLOTS, rows(z * TOK, TOK), :]

        either(k, WIDE_BACK, wide, narrow)

    def z_back(i):
        return ((z + NZ - i) % NZ) * TOK

    def st_v(k):
        def wide(k):
            w = v_y(k)
            all_arrived(v_e(k, pl.ds(NZ * TOK, (NZ - 1) * TOK)), bzrs.at[k])
            total = zc[W + w, :, NZ * TOK : (NZ + 1) * TOK, :].astype(F32)
            for i in range(1, NZ):
                total += zc[W + w, :, (NZ + i) * TOK : (NZ + i + 1) * TOK, :].astype(F32)
            xsc[w] = total.astype(BF16)
            for i in (2, 1, 3):
                vx_copy(i, k).start()
            xrc[w, x] = xsc[w, x]

        def narrow(k):
            all_arrived(zr.at[seven, cols(k)], bzrs.at[k])
            total = zr[0:TOK, cols(k)].astype(F32)
            for i in range(1, NZ):
                total += zr[i * TOK : (i + 1) * TOK, cols(k)].astype(F32)

            @pl.when(k < NH)
            def _():
                mixed_ref[:, cols(k)] = total.astype(BF16)

            @pl.when(k >= NH)
            def _():
                tgrad_ref[:, cols(k - NH)] = total.astype(BF16)

        either(k, WIDE_BACK, wide, narrow)

    def st_u(k):
        @pl.when(among(k, WIDE_BACK))
        def _():
            w = v_y(k)
            for i in range(1, NX):
                part = xrc.at[w, (x + NX - i) % NX]
                arrived(part, vxss.at[i - 1, w], vxrs.at[i - 1, w], at_x(i))
            total = xrc[w, 0].astype(F32)
            for i in range(1, NX):
                total += xrc[w, i].astype(F32)
            tgrad_ref[:, cols(k - NH)] = total.astype(BF16)
            for i in range(1, NX):
                vx_copy(i, k).wait_send()

    def st_hy(k):
        @pl.when(jnp.logical_not(among(k, WIDE_BACK)))
        def _():
            all_sent(ybuf.at[0, three], byss.at[k])

    def st_he(k):
        either(k, WIDE_BACK, lambda k: ve_copy(k).wait_send(), lambda k: be_copy(k).wait_send())

    def st_hz(k):
        def wide(k):
            all_sent(zc.at[0, :, seven], bzss.at[k])

        def narrow(k):
            all_sent(zs.at[0, seven], bzss.at[k])

        either(k, WIDE_BACK, wide, narrow)

    def w_copies(k):
        return [
            pltpu.make_async_copy(stage.at[n], ref.at[:, cols(k)], wsem.at[n])
            for n, ref in enumerate((dwg_hbm, dwu_hbm, dwd_hbm))
        ]

    def st_weights(k):
        @pl.when(k == 0)
        def _():
            hid_t[...] = hid[...].astype(F32).T.astype(BF16)
            dgp_t[...] = dgp[...].astype(F32).T.astype(BF16)
            dup_t[...] = dup[...].astype(F32).T.astype(BF16)

        @pl.when(k >= 1)
        def _():
            for cp in w_copies(k - 1):
                cp.wait()

        part = all_rows(k)
        stage[0] = nn(dgp_t[...], part).astype(BF16)
        stage[1] = nn(dup_t[...], part).astype(BF16)
        stage[2] = nn(hid_t[...], all_rows(k + NH)).astype(BF16)
        for cp in w_copies(k):
            cp.start()

    def ge_copy():
        return remote(gsend, grecv, gess, gers, other)

    def gz_copy(i):
        src = gz_s.at[rows(((z + i) % NZ) * TOK, TOK)]
        return remote(src, gz_r.at[rows(z * TOK, TOK)], gzss.at[i - 1], gzrs.at[i - 1], at_z(i))

    def st_gate(k):
        lanes = iota((ROWS, 128), 1)
        j, _, _ = row_parts(iota((ROWS, 128), 0))
        hit = jnp.where(lanes == z * (NY * NC) + NC * j + c, 1.0, 0.0).astype(BF16)
        a, b, d = split3(gacc[...] * dmat_t[x].astype(F32))
        gtmp[...] = nn(a, hit) + nn(b, hit) + nn(d, hit)
        gsend[...] = gtmp[oth_part, :]
        ge_copy().start()

    def st_gate_z(k):
        ge_copy().wait_recv()
        gz_s[...] = gtmp[me_part, :] + grecv[...]
        for i in z_order:
            gz_copy(i).start()
        gz_r[rows(z * TOK, TOK), :] = gz_s[rows(z * TOK, TOK), :]

    def st_gate_end(k):
        for i in range(1, NZ):
            arrived(gz_r.at[rows(z_back(i), TOK)], gzss.at[i - 1], gzrs.at[i - 1], at_z(i))
        total = gz_r[0:TOK, :]
        for i in range(1, NZ):
            total += gz_r[i * TOK : (i + 1) * TOK, :]
        own = meta[x, mine, :]
        lanes = iota((TOK, 128), 1).astype(F32)
        lane8 = iota((TOK, 8), 1)
        res = jnp.zeros((TOK, 8), F32)
        for k in range(8):
            val = jnp.sum(jnp.where(own[:, k : k + 1] == lanes, total, 0.0), axis=1, keepdims=True)
            res = jnp.where(lane8 == k, val, res)
        eye8 = jnp.where(iota((8, 8), 0) == iota((8, 8), 1), 1.0, 0.0).astype(BF16)
        r3 = split3(res)
        ggrad_ref[...] = nt(eye8, r3[0]) + nt(eye8, r3[1]) + nt(eye8, r3[2])
        ge_copy().wait_send()
        for i in range(1, NZ):
            gz_copy(i).wait_send()

    def guarded(fn, k, low=0, high=N):
        @pl.when((k >= low) & (k < high))
        def _():
            fn(k)

    START = 4
    for i in z_order:
        mz_copy(i).start()
    for k in range(3):
        for i in z_order:
            z_copy(i, k).start()
    for i in range(1, NZ):
        arrived(meta.at[x, z_part(i)], mzss.at[i - 1], mzrs.at[i - 1], at_z(i))
    me_copy.start()
    guarded(st_x, START + 2 + 0 * x)
    st_b(0)
    g_acc[...] = jnp.zeros_like(g_acc)
    u_acc[...] = jnp.zeros_like(u_acc)
    d_acc[...] = jnp.zeros_like(d_acc)
    gacc[...] = jnp.zeros_like(gacc)
    arrived(meta.at[x, oth_part], mess, mers, other)
    st_b(1)
    for i in (2, 1, 3):
        mx_copy(i).start()
    route(x, True)
    loads[2].wait()
    loads[3].wait()
    loads[4].wait()

    def step(i, carry):
        guarded(st_x, i + 3)
        guarded(st_az, i + 2)
        guarded(st_ring(1), i + 1)
        guarded(st_ring(2), i)
        guarded(st_ring(3), i - 1)
        guarded(st_an, i - 1)
        guarded(st_gy, i - 7)
        guarded(st_d, i - 5)
        guarded(st_c, i - 4)
        guarded(st_b, i - 3, 2)
        guarded(st_e, i - 6)
        guarded(route_other, i - 4, 0, NX - 1)
        guarded(st_f, i - 7)
        guarded(st_g, i - 10)
        k = i - 6 - NH
        guarded(st_w, k - PSLOTS)
        guarded(st_p, k)
        guarded(st_q, k - 1)
        guarded(st_hy, k - 5)
        guarded(st_r, k - 2)
        guarded(st_s, k - 4)
        guarded(st_t, k - 5)
        guarded(st_gate, k - 4 - NH, 0, 1)
        guarded(st_gate_z, k - 5 - NH, 0, 1)
        guarded(st_gate_end, k - 7 - NH, 0, 1)
        guarded(st_v, k - 7)
        guarded(st_he, k - 7)
        guarded(st_hz, k - 8)
        guarded(st_u, k - 9)
        guarded(st_weights, k - NH - 4, 0, NH)
        return carry

    lax.fori_loop(START, N + NH + 6 + 9, step, 0)
    for i in range(1, NZ):
        mz_copy(i).wait_send()
    me_copy.wait_send()
    for i in range(1, NX):
        mx_copy(i).wait_send()
    for cp in w_copies(NH - 1):
        cp.wait()


def settle(*refs):
    for i in range(len(refs) // 2):
        refs[len(refs) // 2 + i][...] = refs[i][...]


def body(tokens, cotangent, gate_prob, expert_ids, placement, gate_weight, up_weight, down_weight):
    toks, D = tokens.shape
    FQ = gate_weight.shape[1]
    N = 2 * D // CW
    R = NX * ROWS
    NT = NZ * TOK
    WO, WB = len(WIDE_OUT), len(WIDE_BACK)
    dma = pltpu.SemaphoreType.DMA
    vm = pltpu.VMEM
    vspec = pl.BlockSpec(memory_space=pltpu.VMEM)
    aspec = pl.BlockSpec(memory_space=pl.ANY)
    scratch = [
        vm((GROUP, 2 * D), BF16),
        vm((WO, NX, GROUP, CW), BF16),
        vm((SLOTS, ROWS, CW), BF16),
        vm((2, NX, ROWS, CW), BF16),
        vm((NX, ROWS, 2 * D), BF16),
        vm((FQ, D), BF16), vm((FQ, D), BF16), vm((FQ, D), BF16),
        vm((PSLOTS, NX, ROWS, CW), BF16),
        vm((ROWS, 2 * D), BF16),
        vm((ROWS, 2 * D), BF16),
        vm((ROWS, 2 * D), BF16),
        vm((SLOTS, ROWS, CW), BF16),
        vm((ROWS, 2 * D), BF16),
        vm((SLOTS, NT, CW), BF16),
        vm((NT, 2 * D), BF16),
        vm((SLOTS, NT, CW), BF16),
        vm((NT, 2 * D), BF16),
        vm((WB, NX, NT, CW), BF16),
        vm((WB, NX, NT, CW), BF16),
        vm((WB, NX, TOK, CW), BF16),
        vm((WB, NX, TOK, CW), BF16),
        vm((R, FQ), F32), vm((R, FQ), F32), vm((R, FQ), F32),
        vm((R, FQ), BF16), vm((R, FQ), BF16), vm((R, FQ), BF16),
        vm((FQ, R), BF16), vm((FQ, R), BF16), vm((FQ, R), BF16),
        vm((3, FQ, CW), BF16),
        vm((NX, GROUP, 128), F32),
        vm((NX, ROWS, GROUP), BF16),
        vm((NX, GROUP, ROWS), BF16),
        vm((GROUP, ROWS), BF16), vm((GROUP, ROWS), BF16),
        vm((NX, ROWS, 128), F32),
        vm((GROUP, ROWS), F32),
        vm((GROUP, 128), F32),
        vm((NT, 128), F32), vm((NT, 128), F32),
        vm((NT, 128), F32), vm((NT, 128), F32),
        dma((5,)),
        dma((1, N)), dma((NZ - 1, N)), dma((N,)), dma((N,)),
        dma((N,)), dma((N,)), dma((N,)), dma((4, N)),
        dma((N,)), dma((6, N)), dma((N,)), dma((N,)),
        dma((N,)), dma((N,)), dma((N,)), dma((N,)),
        dma((NX - 1, WO)), dma((NX - 1, WO)), dma((NX - 1, WB)), dma((NX - 1, WB)),
        dma((NZ - 1,)), dma((NZ - 1,)), dma(()), dma(()), dma((NX - 1,)), dma((NX - 1,)),
        dma(()), dma(()), dma((NZ - 1,)), dma((NZ - 1,)), dma((3,)),
    ]
    shapes = (
        jax.ShapeDtypeStruct((toks, D), BF16),
        jax.ShapeDtypeStruct((toks, D), BF16),
        jax.ShapeDtypeStruct(gate_prob.shape[::-1], F32),
        jax.ShapeDtypeStruct((FQ, D), BF16),
        jax.ShapeDtypeStruct((FQ, D), BF16),
        jax.ShapeDtypeStruct((FQ, D), BF16),
    )
    outs = pl.pallas_call(
        kernel,
        out_shape=shapes,
        in_specs=[aspec, aspec, vspec, vspec, vspec, aspec, aspec, aspec],
        out_specs=(vspec, vspec, vspec, aspec, aspec, aspec),
        scratch_shapes=scratch,
        compiler_params=pltpu.CompilerParams(
            collective_id=0, has_side_effects=True, vmem_limit_bytes=63 * 2**20
        ),
        cost_estimate=pl.CostEstimate(
            flops=9 * 2 * R * FQ * D, bytes_accessed=6 * FQ * D * 2, transcendentals=R * FQ
        ),
        name="moe_layer",
    )(
        tokens, cotangent, expert_ids.T, gate_prob.T, placement.reshape(1, -1),
        gate_weight[0], up_weight[0], down_weight[0],
    )
    steps = 2
    wide = pl.BlockSpec((toks, D // steps), lambda i: (0, i))
    grads = pl.BlockSpec((FQ, D // steps), lambda i: (0, i))
    specs = (wide, wide, pl.BlockSpec(gate_prob.shape[::-1], lambda i: (0, 0)), grads, grads, grads)
    outs = pl.pallas_call(
        settle, out_shape=shapes, grid=(steps,), in_specs=list(specs), out_specs=specs, name="settle"
    )(*outs)
    mixed, token_grad, gate_grad, dwg, dwu, dwd = outs
    return mixed, token_grad, gate_grad.T, dwg[None], dwu[None], dwd[None]


def solution(mesh):
    rows_spec = P(("dp", "expert"), None)
    weight_spec = P("expert", "dp", None)
    return jax.shard_map(
        body,
        mesh=mesh,
        in_specs=(rows_spec,) * 4 + (P(),) + (weight_spec,) * 3,
        out_specs=(rows_spec,) * 3 + (weight_spec,) * 3,
        check_vma=False,
    )
```
